512 devices in a mesh: rows: 128 (over y, z, core), grp: 4 (over x).
Axes of the slice: x: 4, y: 4, z: 16, core: 2. Of those that a mesh axis runs over, the one named last changes fastest.
Arguments:
- embeddings: float32 [114688, 4096], P(('rows', 'grp')), may hold values from -108 to 108
- test_matrix: bfloat16 [4096, 128], replicated, may hold values from -0.09375 to 0.09375
Outputs:
- basis: float32 [114688, 128], P(('rows', 'grp'))
- right_basis: float32 [4096, 128], P(('rows', 'grp'))
- factor: float32 [128, 128], replicated
The draws below stay inside these ranges and needn't reach their ends.
All inputs are finite; a program needn't handle non-finite values.
Results may differ from the reference program's by a relative error of at most 0.0003.
Values sent between devices are 32-bit elements; how exact they have to be, the bound alone decides.
No kernel may reach another device: no remote copies, remote signals or barrier semaphores. Data moves between devices by JAX's collectives and lax.ppermute only.
A program may use at most 64 MiB of HBM per device.

```python
import math
import jax
import jax.numpy as jnp
from jax import lax

D = 4096
K = 128
ROWS = 114688


def draw_embeddings(key, part):
    key = jax.random.fold_in(key, 11)
    first_key, second_key, third_key = jax.random.split(key, 3)
    position = jnp.arange(ROWS, dtype=jnp.float32)[:, None] / ROWS
    growth = jnp.exp(math.log(3.0) * position)
    row_scale = jnp.exp(jax.random.uniform(second_key, (ROWS, 1), jnp.float32, 0.0, math.log(10.0)))
    column_scale = jnp.exp(jax.random.uniform(third_key, (1, D), jnp.float32, math.log(0.5), math.log(2.0)))
    entries = jnp.clip(jax.random.normal(first_key, (ROWS, D), jnp.float32), -6.0, 6.0)
    return 0.3 * entries * column_scale * row_scale * growth


def centred(own_key, extent, deviation, limit, held_as=jnp.bfloat16):
    return jnp.clip(deviation * jax.random.normal(own_key, extent, jnp.float32), -limit, limit).astype(held_as)


def setup_inputs(seed: int = 0) -> dict:
    key_list = jax.random.split(jax.random.key(seed), 3)
    embeddings = draw_embeddings(jax.random.fold_in(key_list[2], 71), 0)
    test_matrix = centred(key_list[1], (D, K), D ** -0.5, 0.09375)
    return dict(embeddings=embeddings, test_matrix=test_matrix)


def gram_of(values, divisor):
    product = lax.dot_general(values.astype(jnp.float32), values.astype(jnp.float32), (((0,), (0,)), ((), ())), precision=lax.Precision.HIGHEST, preferred_element_type=jnp.float32)
    return product / divisor

def lower_solve(lower, values):
    return lax.linalg.triangular_solve(lower, values, left_side=False, lower=True, transpose_a=True)

def reference(embeddings, test_matrix):
    total_rows = embeddings.shape[0]
    width = embeddings.shape[1]
    sketch = jnp.dot(embeddings.astype(jnp.float32), test_matrix.astype(jnp.float32), precision=lax.Precision.HIGHEST, preferred_element_type=jnp.float32)
    lower_first = jnp.linalg.cholesky(gram_of(sketch, total_rows))
    basis = lower_solve(lower_first, sketch)
    loadings = lax.dot_general(embeddings.astype(jnp.float32), basis.astype(jnp.float32), (((0,), (0,)), ((), ())), precision=lax.Precision.HIGHEST, preferred_element_type=jnp.float32)
    factor = jnp.linalg.cholesky(gram_of(loadings, width))
    right_basis = lower_solve(factor, loadings)
    return (basis, right_basis, factor)
```

```python
import jax
import jax.numpy as jnp
from jax import lax
from jax.sharding import Mesh, PartitionSpec as P

HIGHEST = lax.Precision.HIGHEST
AXES = ("y", "z", "core", "x")


def exchange(values, axes):
    return lax.all_to_all(values, axes, 0, 0, tiled=False)


def reduce_scatter(values, axes):
    parts = lax.axis_size(axes)
    blocks = values.reshape((parts, values.shape[0] // parts) + values.shape[1:])
    return jnp.sum(exchange(blocks, axes), axis=0)


def gather(values, axes):
    parts = lax.axis_size(axes)
    copies = jnp.broadcast_to(values[None], (parts,) + values.shape)
    blocks = exchange(copies, axes)
    return blocks.reshape((parts * values.shape[0],) + values.shape[1:])


def lower_solve(lower, values):
    return lax.linalg.triangular_solve(lower, values, left_side=False, lower=True, transpose_a=True)


def dot(left, right, left_dim, right_dim):
    return lax.dot_general(
        left,
        right,
        (((left_dim,), (right_dim,)), ((), ())),
        precision=HIGHEST,
        preferred_element_type=jnp.float32,
    )


def per_device(embeddings, test_matrix):
    devices_all = lax.axis_size(AXES)
    total_rows = embeddings.shape[0] * devices_all
    width = embeddings.shape[1]
    own_rows = width // devices_all
    test = test_matrix.astype(jnp.float32)
    sketch = dot(embeddings, test, 1, 0)
    image = dot(embeddings, sketch, 0, 0)
    image = reduce_scatter(image, "core")
    image = reduce_scatter(image, ("x", "y"))
    image = reduce_scatter(image, "z")
    image = gather(image, "z")
    image = gather(image, ("x", "y"))
    image = gather(image, "core")
    lower_first = jnp.linalg.cholesky(dot(test, image, 0, 0) / total_rows, symmetrize_input=False)
    basis = lower_solve(lower_first, sketch)
    loadings = lower_solve(lower_first, image)
    factor = jnp.linalg.cholesky(dot(loadings, loadings, 0, 0) / width, symmetrize_input=False)
    own = lax.dynamic_slice_in_dim(loadings, lax.axis_index(AXES) * own_rows, own_rows, 0)
    right_basis = lower_solve(factor, own)
    return (basis, right_basis, factor)


def solution(mesh):
    fine = Mesh(mesh.devices.reshape(4, 16, 2, 4), AXES)
    return jax.shard_map(
        per_device,
        mesh=fine,
        in_specs=(P(AXES, None), P()),
        out_specs=(P(AXES, None), P(AXES, None), P()),
        check_vma=False,
    )
```

```python
import functools

import jax
import jax.numpy as jnp
from jax import lax
from jax.experimental import pallas as pl
from jax.experimental.pallas import tpu as pltpu
from jax.sharding import Mesh, PartitionSpec as P

AXES = ("y", "z", "core", "x")
CHUNKS = 8
PANEL = 32
LANES = 128
F32, BF16 = jnp.float32, jnp.bfloat16
VMEM_LIMIT = 60 * 1024 * 1024


def dot(left, right, right_dim=0):
    return lax.dot_general(left, right, (((1,), (right_dim,)), ((), ())), preferred_element_type=F32)


def split(values):
    first = values.astype(BF16)
    rest = values - first.astype(F32)
    second = rest.astype(BF16)
    return first, second, (rest - second.astype(F32)).astype(BF16)


def dot_split(left, right):
    rows = left[0].shape[0]
    high = dot(jnp.concatenate(left, axis=0), right[0])
    middle = dot(jnp.concatenate(left[:2], axis=0), right[1])
    low = dot(left[0], right[2])
    small = high[2 * rows :] + middle[rows:] + low
    return high[:rows] + (high[rows : 2 * rows] + middle[:rows] + small)


def image_kernel(core_ref, emb_hbm, test_hbm, sketch_ref, keep_ref, send_ref, emb, test, terms, sems):
    rows, columns = emb.shape[1], emb.shape[2]
    copies = []
    for c in range(CHUNKS):
        span = pl.ds(c * columns, columns)
        copies.append(
            (
                pltpu.make_async_copy(emb_hbm.at[:, span], emb.at[c], sems.at[0, c]),
                pltpu.make_async_copy(test_hbm.at[span], test.at[c], sems.at[1, c]),
            )
        )
    for pair in copies:
        for copy in pair:
            copy.start()
    sketch = jnp.zeros((rows, LANES), F32)
    for c in range(CHUNKS):
        for copy in copies[c]:
            copy.wait()
        parts = split(emb[c])
        for t in range(3):
            terms[t, c] = parts[t]
        product = dot(jnp.concatenate(parts, axis=0), test[c])
        sketch += product[:rows] + (product[rows : 2 * rows] + product[2 * rows :])
    sketch_ref[...] = sketch
    left = split(sketch.T)
    per_chunk = columns // LANES
    core = core_ref[0]
    for out, half in ((send_ref, 1 - core), (keep_ref, core)):
        for i in range(CHUNKS // 2):
            c = half * (CHUNKS // 2) + i
            part = dot_split(left, [terms[t, c] for t in range(3)])
            for b in range(per_chunk):
                out[i * per_chunk + b] = part[:, b * LANES : (b + 1) * LANES]


def local_image(core, embeddings, test_matrix):
    rows, width = embeddings.shape
    columns = width // CHUNKS
    blocks = jax.ShapeDtypeStruct((width // (2 * LANES), LANES, LANES), F32)
    vmem = pl.BlockSpec(memory_space=pltpu.VMEM)
    return pl.pallas_call(
        image_kernel,
        out_shape=[jax.ShapeDtypeStruct((rows, LANES), F32), blocks, blocks],
        in_specs=[
            pl.BlockSpec(memory_space=pltpu.SMEM),
            pl.BlockSpec(memory_space=pl.ANY),
            pl.BlockSpec(memory_space=pl.ANY),
        ],
        out_specs=[vmem] * 3,
        scratch_shapes=[
            pltpu.VMEM((CHUNKS, rows, columns), F32),
            pltpu.VMEM((CHUNKS, columns, LANES), BF16),
            pltpu.VMEM((3, CHUNKS, rows, columns), BF16),
            pltpu.SemaphoreType.DMA((2, CHUNKS)),
        ],
        compiler_params=pltpu.CompilerParams(vmem_limit_bytes=VMEM_LIMIT),
        cost_estimate=pl.CostEstimate(flops=2 * 9 * rows * width * LANES, bytes_accessed=4 * rows * width, transcendentals=0),
        name="local_image",
    )(core, embeddings, test_matrix)


def over_sublanes(tile, row):
    return jnp.broadcast_to(tile[row : row + 1], tile.shape)


def over_lanes(tile, lane):
    return jnp.broadcast_to(tile[:, lane : lane + 1], tile.shape)


def eliminate(a, b, first_lane):
    sublane = lax.broadcasted_iota(jnp.int32, (8, LANES), 0)
    for g in range(len(a)):
        column = {q: [over_lanes(a[q], first_lane + 8 * g + k) for k in range(8)] for q in range(g, len(a))}
        for i in range(8):
            inverse = 1.0 / over_sublanes(column[g][i], i)
            row_a, row_b = over_sublanes(a[g], i), over_sublanes(b[g], i)
            pivots = [over_sublanes(column[g][k], i) for k in range(8)]
            for q in range(g, len(a)):
                factor = column[q][i] * inverse
                if q == g:
                    if i == 7:
                        continue
                    factor = jnp.where(sublane > i, factor, 0.0)
                for k in range(i + 1, 8):
                    column[q][k] = column[q][k] - factor * pivots[k]
                a[q] = a[q] - factor * row_a
                b[q] = b[q] - factor * row_b


def factorize(gram):
    size = gram.shape[0]
    tiles = lambda value: [value[8 * t : 8 * t + 8] for t in range(PANEL // 8)]
    row = lax.broadcasted_iota(jnp.int32, (size, size), 0)
    column = lax.broadcasted_iota(jnp.int32, (size, size), 1)
    other = jnp.where(row == column, 1.0, 0.0).astype(F32)
    uppers, inverses = [], []
    for start in range(0, size, PANEL):
        a, b = tiles(gram), tiles(other)
        eliminate(a, b, start)
        a, b = jnp.concatenate(a, axis=0), jnp.concatenate(b, axis=0)
        here = row[start : start + PANEL]
        lanes = column[start : start + PANEL]
        scale = lax.rsqrt(jnp.sum(jnp.where(here == lanes, a, 0.0), axis=1, keepdims=True))
        upper, inverse = jnp.where(lanes >= here, a * scale, 0.0), b * scale
        uppers.append(upper)
        inverses.append(inverse)
        if start + PANEL < size:
            below = split(upper.T[start + PANEL :])
            gram = gram[PANEL:] - dot_split(below, split(upper))
            other = other[PANEL:] - dot_split(below, split(inverse))
    return jnp.concatenate(uppers, axis=0), jnp.concatenate(inverses, axis=0)


def finish_kernel(
    total_rows, place_ref, mine_ref, other_ref, sketch_ref, test_ref,
    basis_ref, right_ref, factor_ref, loadings, turned,
):
    blocks = mine_ref.shape[0]
    group = 4
    core = place_ref[0]
    halves = ((mine_ref, core), (other_ref, 1 - core))

    def wide(ref, first):
        return jnp.concatenate([ref[first + b] for b in range(group)], axis=1)

    partial = []
    for ref, half in halves:
        total = jnp.zeros((LANES, LANES), F32)
        for first in range(0, blocks, group):
            terms = jnp.concatenate(split(wide(ref, first)), axis=0)
            offset = pl.multiple_of((half * blocks + first) * LANES, group * LANES)
            product = dot(terms, test_ref[pl.ds(offset, group * LANES), :])
            total += product[:LANES] + (product[LANES : 2 * LANES] + product[2 * LANES :])
        partial.append(total)
    gram = (partial[0] + partial[1]) * (0.5 / total_rows)
    _, inverse = factorize(gram + gram.T)
    left = split(inverse)

    partial = []
    for h, (ref, _) in enumerate(halves):
        total = jnp.zeros((LANES, LANES), F32)
        for first in range(0, blocks, group):
            values = dot_split(left, split(wide(ref, first)))
            for b in range(group):
                loadings[h * blocks + first + b] = values[:, b * LANES : (b + 1) * LANES]
            terms = split(values)
            product = dot(jnp.concatenate(terms, axis=0), terms[0], 1)
            cross = product[LANES : 2 * LANES] + product[2 * LANES :]
            total += product[:LANES] + (cross + cross.T + dot(terms[1], terms[1], 1))
        partial.append(total)
    upper, second = factorize((partial[0] + partial[1]) / (2 * blocks * LANES))
    factor_ref[...] = upper.T

    basis_ref[...] = dot_split(split(sketch_ref[...]), split(inverse.T))
    turned[...] = dot_split(split(second), split(loadings[place_ref[1]])).T
    right_ref[...] = turned[pl.ds(pl.multiple_of(place_ref[2], 8), right_ref.shape[0]), :]


def finish(place, mine, other, sketch, test_matrix, total_rows, own_rows):
    vmem = pl.BlockSpec(memory_space=pltpu.VMEM)
    return pl.pallas_call(
        functools.partial(finish_kernel, total_rows),
        out_shape=[
            jax.ShapeDtypeStruct(sketch.shape, F32),
            jax.ShapeDtypeStruct((own_rows, LANES), F32),
            jax.ShapeDtypeStruct((LANES, LANES), F32),
        ],
        in_specs=[pl.BlockSpec(memory_space=pltpu.SMEM)] + [vmem] * 4,
        out_specs=[vmem] * 3,
        scratch_shapes=[
            pltpu.VMEM((2 * mine.shape[0], LANES, LANES), F32),
            pltpu.VMEM((LANES, LANES), F32),
        ],
        compiler_params=pltpu.CompilerParams(vmem_limit_bytes=VMEM_LIMIT),
        name="finish",
    )(place, mine, other, sketch, test_matrix)


def exchange(values, axes):
    return lax.all_to_all(values, axes, 0, 0, tiled=False)


def scatter_sum(values, axes):
    parts = lax.axis_size(axes)
    blocks = values.reshape((parts, values.shape[0] // parts) + values.shape[1:])
    return jnp.sum(exchange(blocks, axes), axis=0)


def gather(values, axes):
    parts = lax.axis_size(axes)
    blocks = exchange(jnp.broadcast_to(values[None], (parts,) + values.shape), axes)
    return blocks.reshape((parts * values.shape[0],) + values.shape[1:])


def swap_cores(values):
    return lax.ppermute(values, "core", [(0, 1), (1, 0)])


def per_device(embeddings, test_matrix):
    devices_all = lax.axis_size(AXES)
    rows, width = embeddings.shape
    own_rows = width // devices_all
    core = lax.axis_index("core")
    sketch, keep, send = local_image(core.reshape(1), embeddings, test_matrix)
    image = keep + swap_cores(send)
    block = scatter_sum(image, ("x", "y")).reshape(LANES, LANES)
    block = gather(scatter_sum(block, "z"), "z")
    mine = gather(block[None], ("x", "y"))
    other = swap_cores(mine)
    first = lax.axis_index(AXES) * own_rows
    half_blocks = mine.shape[0]
    own_block = first // LANES
    slot = jnp.where(own_block // half_blocks == core, 0, half_blocks) + own_block % half_blocks
    place = jnp.stack([core, slot, first % LANES])
    basis, right_basis, factor = finish(place, mine, other, sketch, test_matrix, rows * devices_all, own_rows)
    return (basis, right_basis, factor)


def solution(mesh):
    fine = Mesh(mesh.devices.reshape(4, 16, 2, 4), AXES)
    return jax.shard_map(
        per_device,
        mesh=fine,
        in_specs=(P(AXES, None), P()),
        out_specs=(P(AXES, None), P(AXES, None), P()),
        check_vma=False,
    )
```

```python
import functools

import jax
import jax.numpy as jnp
from jax import lax
from jax.experimental import pallas as pl
from jax.experimental.pallas import tpu as pltpu
from jax.sharding import Mesh, PartitionSpec as P

AXES = ("y", "z", "core", "x")
CHUNKS = 4
STEP = 512
PANEL = 32
LANES = 128
F32, BF16 = jnp.float32, jnp.bfloat16
VMEM_LIMIT = 24 * 1024 * 1024


def dot(left, right, right_dim=0):
    return lax.dot_general(left, right, (((1,), (right_dim,)), ((), ())), preferred_element_type=F32)


def split(values):
    first = values.astype(BF16)
    rest = values - first.astype(F32)
    second = rest.astype(BF16)
    return first, second, (rest - second.astype(F32)).astype(BF16)


def dot_split(left, right):
    rows = left[0].shape[0]
    high = dot(jnp.concatenate(left, axis=0), right[0])
    middle = dot(jnp.concatenate(left[:2], axis=0), right[1])
    low = dot(left[0], right[2])
    small = high[2 * rows :] + middle[rows:] + low
    return high[:rows] + (high[rows : 2 * rows] + middle[:rows] + small)


def image_blocks(left, right, out, first):
    part = dot(left[0], right[0]) + (
        (dot(left[1], right[0]) + dot(left[0], right[1]))
        + (dot(left[2], right[0]) + dot(left[1], right[1]) + dot(left[0], right[2]))
    )
    for b in range(part.shape[1] // LANES):
        out[first + b] = part[:, b * LANES : (b + 1) * LANES]


def sketch_kernel(core_ref, emb_hbm, test_hbm, sketch_ref, send_ref, keep_terms, emb, test, send_terms, sems):
    rows, width = emb.shape
    columns = width // CHUNKS
    core = core_ref[0]
    copies = []
    for c in range(CHUNKS):
        there = pl.multiple_of(lax.rem(core * (width // 2) + c * columns, width), columns)
        here = pl.ds(c * columns, columns)
        copies.append(
            (
                pltpu.make_async_copy(emb_hbm.at[:, pl.ds(there, columns)], emb.at[:, here], sems.at[0, c]),
                pltpu.make_async_copy(test_hbm.at[pl.ds(there, columns)], test.at[here], sems.at[1, c]),
            )
        )
    for pair in copies:
        for copy in pair:
            copy.start()
    sketch = jnp.zeros((rows, LANES), F32)
    for c in range(CHUNKS):
        for copy in copies[c]:
            copy.wait()
        here = slice(c * columns, (c + 1) * columns)
        parts = split(emb[:, here])
        terms, first = (keep_terms, 0) if c < CHUNKS // 2 else (send_terms, width // 2)
        for t in range(3):
            terms[t, :, here.start - first : here.stop - first] = parts[t]
            sketch += dot(parts[t], test[here])
    sketch_ref[...] = sketch
    left = split(sketch.T)
    for start in range(0, width // 2, STEP):
        image_blocks(left, [send_terms[t, :, start : start + STEP] for t in range(3)], send_ref, start // LANES)


def keep_kernel(sketch_ref, keep_terms, keep_ref):
    left = split(sketch_ref[...].T)
    for start in range(0, keep_terms.shape[2], STEP):
        image_blocks(left, [keep_terms[t, :, start : start + STEP] for t in range(3)], keep_ref, start // LANES)


def local_sketch(core, embeddings, test_matrix):
    rows, width = embeddings.shape
    half = width // 2
    vmem = pl.BlockSpec(memory_space=pltpu.VMEM)
    return pl.pallas_call(
        sketch_kernel,
        out_shape=[
            pltpu.VMEM((rows, LANES), F32),
            pltpu.VMEM((half // LANES, LANES, LANES), F32),
            pltpu.VMEM((3, rows, half), BF16),
        ],
        in_specs=[
            pl.BlockSpec(memory_space=pltpu.SMEM),
            pl.BlockSpec(memory_space=pltpu.HBM),
            pl.BlockSpec(memory_space=pltpu.HBM),
        ],
        out_specs=[vmem] * 3,
        scratch_shapes=[
            pltpu.VMEM((rows, width), F32),
            pltpu.VMEM((width, LANES), BF16),
            pltpu.VMEM((3, rows, half), BF16),
            pltpu.SemaphoreType.DMA((2, CHUNKS)),
        ],
        compiler_params=pltpu.CompilerParams(vmem_limit_bytes=VMEM_LIMIT),
        cost_estimate=pl.CostEstimate(flops=12 * rows * width * LANES, bytes_accessed=4 * rows * width, transcendentals=0),
        name="local_sketch",
    )(
        core,
        pltpu.with_memory_space_constraint(embeddings, pltpu.HBM),
        pltpu.with_memory_space_constraint(test_matrix, pltpu.HBM),
    )


def keep_image(sketch, keep_terms):
    rows, half = keep_terms.shape[1:]
    vmem = pl.BlockSpec(memory_space=pltpu.VMEM)
    return pl.pallas_call(
        keep_kernel,
        out_shape=pltpu.VMEM((half // LANES, LANES, LANES), F32),
        in_specs=[vmem] * 2,
        out_specs=vmem,
        compiler_params=pltpu.CompilerParams(vmem_limit_bytes=VMEM_LIMIT),
        cost_estimate=pl.CostEstimate(flops=12 * rows * half * LANES, bytes_accessed=6 * rows * half, transcendentals=0),
        name="keep_image",
    )(sketch, keep_terms)


def over_sublanes(tile, row):
    return jnp.broadcast_to(tile[row : row + 1], tile.shape)


def over_lanes(tile, lane):
    return jnp.broadcast_to(tile[:, lane : lane + 1], tile.shape)


def eliminate(a, b, first_lane):
    sublane = lax.broadcasted_iota(jnp.int32, (8, LANES), 0)
    for g in range(len(a)):
        column = {q: [over_lanes(a[q], first_lane + 8 * g + k) for k in range(8)] for q in range(g, len(a))}
        for i in range(8):
            inverse = 1.0 / over_sublanes(column[g][i], i)
            row_a, row_b = over_sublanes(a[g], i), over_sublanes(b[g], i)
            pivots = [over_sublanes(column[g][k], i) for k in range(8)]
            for q in range(g, len(a)):
                factor = column[q][i] * inverse
                if q == g:
                    if i == 7:
                        continue
                    factor = jnp.where(sublane > i, factor, 0.0)
                for k in range(i + 1, 8):
                    column[q][k] = column[q][k] - factor * pivots[k]
                a[q] = a[q] - factor * row_a
                b[q] = b[q] - factor * row_b


def factorize(gram):
    size = gram.shape[0]
    tiles = lambda value: [value[8 * t : 8 * t + 8] for t in range(PANEL // 8)]
    row = lax.broadcasted_iota(jnp.int32, (size, size), 0)
    column = lax.broadcasted_iota(jnp.int32, (size, size), 1)
    other = jnp.where(row == column, 1.0, 0.0).astype(F32)
    uppers, inverses = [], []
    for start in range(0, size, PANEL):
        a, b = tiles(gram), tiles(other)
        eliminate(a, b, start)
        a, b = jnp.concatenate(a, axis=0), jnp.concatenate(b, axis=0)
        here = row[start : start + PANEL]
        lanes = column[start : start + PANEL]
        scale = lax.rsqrt(jnp.sum(jnp.where(here == lanes, a, 0.0), axis=1, keepdims=True))
        upper, inverse = jnp.where(lanes >= here, a * scale, 0.0), b * scale
        uppers.append(upper)
        inverses.append(inverse)
        if start + PANEL < size:
            below = split(upper.T[start + PANEL :])
            gram = gram[PANEL:] - dot_split(below, split(upper))
            other = other[PANEL:] - dot_split(below, split(inverse))
    return jnp.concatenate(uppers, axis=0), jnp.concatenate(inverses, axis=0)


def finish_kernel(
    total_rows, place_ref, mine_ref, other_ref, sketch_ref, test_ref,
    basis_ref, right_ref, factor_ref, loadings, turned,
):
    blocks = mine_ref.shape[0]
    group = 4
    core = place_ref[0]
    halves = ((mine_ref, core), (other_ref, 1 - core))

    def wide(ref, first):
        return jnp.concatenate([ref[first + b] for b in range(group)], axis=1)

    partial = []
    for ref, half in halves:
        total = jnp.zeros((LANES, LANES), F32)
        for first in range(0, blocks, group):
            terms = jnp.concatenate(split(wide(ref, first)), axis=0)
            offset = pl.multiple_of((half * blocks + first) * LANES, group * LANES)
            product = dot(terms, test_ref[pl.ds(offset, group * LANES), :])
            total += product[:LANES] + (product[LANES : 2 * LANES] + product[2 * LANES :])
        partial.append(total)
    gram = (partial[0] + partial[1]) * (0.5 / total_rows)
    _, inverse = factorize(gram + gram.T)
    left = split(inverse)

    partial = []
    for h, (ref, _) in enumerate(halves):
        total = jnp.zeros((LANES, LANES), F32)
        for first in range(0, blocks, group):
            values = dot_split(left, split(wide(ref, first)))
            for b in range(group):
                loadings[h * blocks + first + b] = values[:, b * LANES : (b + 1) * LANES]
            terms = split(values)
            product = dot(jnp.concatenate(terms, axis=0), terms[0], 1)
            cross = product[LANES : 2 * LANES] + product[2 * LANES :]
            total += product[:LANES] + (cross + cross.T + dot(terms[1], terms[1], 1))
        partial.append(total)
    upper, second = factorize((partial[0] + partial[1]) / (2 * blocks * LANES))
    factor_ref[...] = upper.T

    basis_ref[...] = dot_split(split(sketch_ref[...]), split(inverse.T))
    turned[...] = dot_split(split(second), split(loadings[place_ref[1]])).T
    right_ref[...] = turned[pl.ds(pl.multiple_of(place_ref[2], 8), right_ref.shape[0]), :]


def finish(place, mine, other, sketch, test_matrix, total_rows, own_rows):
    vmem = pl.BlockSpec(memory_space=pltpu.VMEM)
    return pl.pallas_call(
        functools.partial(finish_kernel, total_rows),
        out_shape=[
            jax.ShapeDtypeStruct(sketch.shape, F32),
            jax.ShapeDtypeStruct((own_rows, LANES), F32),
            jax.ShapeDtypeStruct((LANES, LANES), F32),
        ],
        in_specs=[pl.BlockSpec(memory_space=pltpu.SMEM)] + [vmem] * 4,
        out_specs=[vmem] * 3,
        scratch_shapes=[
            pltpu.VMEM((2 * mine.shape[0], LANES, LANES), F32),
            pltpu.VMEM((LANES, LANES), F32),
        ],
        compiler_params=pltpu.CompilerParams(vmem_limit_bytes=VMEM_LIMIT),
        name="finish",
    )(place, mine, other, sketch, test_matrix)


def exchange(values, axes):
    return lax.all_to_all(values, axes, 0, 0, tiled=False)


def scatter_sum(values, axes):
    parts = lax.axis_size(axes)
    blocks = values.reshape((parts, values.shape[0] // parts) + values.shape[1:])
    return jnp.sum(exchange(blocks, axes), axis=0)


def gather(values, axes):
    parts = lax.axis_size(axes)
    blocks = exchange(jnp.broadcast_to(values[None], (parts,) + values.shape), axes)
    return blocks.reshape((parts * values.shape[0],) + values.shape[1:])


def swap_cores(values):
    return lax.ppermute(values, "core", [(0, 1), (1, 0)])


def per_device(embeddings, test_matrix):
    devices_all = lax.axis_size(AXES)
    rows, width = embeddings.shape
    own_rows = width // devices_all
    core = lax.axis_index("core")
    sketch, send, keep_terms = local_sketch(core.reshape(1), embeddings, test_matrix)
    arriving = swap_cores(send)
    image = keep_image(sketch, keep_terms) + arriving
    block = scatter_sum(image, ("x", "y")).reshape(LANES, LANES)
    block = gather(scatter_sum(block, "z"), "z")
    mine = gather(block[None], ("x", "y"))
    other = swap_cores(mine)
    first = lax.axis_index(AXES) * own_rows
    half_blocks = mine.shape[0]
    own_block = first // LANES
    slot = jnp.where(own_block // half_blocks == core, 0, half_blocks) + own_block % half_blocks
    place = jnp.stack([core, slot, first % LANES])
    basis, right_basis, factor = finish(place, mine, other, sketch, test_matrix, rows * devices_all, own_rows)
    return (basis, right_basis, factor)


def solution(mesh):
    fine = Mesh(mesh.devices.reshape(4, 16, 2, 4), AXES)
    return jax.shard_map(
        per_device,
        mesh=fine,
        in_specs=(P(AXES, None), P()),
        out_specs=(P(AXES, None), P(AXES, None), P()),
        check_vma=False,
    )
```

```python
import functools

import jax
import jax.numpy as jnp
from jax import lax
from jax.experimental import pallas as pl
from jax.experimental.pallas import tpu as pltpu
from jax.sharding import Mesh, PartitionSpec as P

AXES = ("y", "z_pair", "z_in_pair", "core", "x")
NEAR = ("x", "y", "z_in_pair")
CHUNKS = 4
STEP = 512
PANEL = 32
LANES = 128
F32, BF16 = jnp.float32, jnp.bfloat16
VMEM_LIMIT = 24 * 1024 * 1024


def dot(left, right, right_dim=0):
    return lax.dot_general(left, right, (((1,), (right_dim,)), ((), ())), preferred_element_type=F32)


def split(values):
    first = values.astype(BF16)
    rest = values - first.astype(F32)
    second = rest.astype(BF16)
    return first, second, (rest - second.astype(F32)).astype(BF16)


def dot_split(left, right, right_dim=0):
    return dot(left[0], right[0], right_dim) + (
        (dot(left[1], right[0], right_dim) + dot(left[0], right[1], right_dim))
        + (dot(left[2], right[0], right_dim) + dot(left[1], right[1], right_dim) + dot(left[0], right[2], right_dim))
    )


def image_blocks(left, right, out, first):
    part = dot(left[0], right[0]) + (
        (dot(left[1], right[0]) + dot(left[0], right[1]))
        + (dot(left[2], right[0]) + dot(left[1], right[1]) + dot(left[0], right[2]))
    )
    for b in range(part.shape[1] // LANES):
        out[first + b] = part[:, b * LANES : (b + 1) * LANES]


def sketch_kernel(core_ref, emb_hbm, test_hbm, sketch_ref, send_ref, keep_terms, emb, test, send_terms, sems):
    rows, width = emb.shape
    columns = width // CHUNKS
    core = core_ref[0]
    copies = []
    for c in range(CHUNKS):
        there = pl.multiple_of(lax.rem(core * (width // 2) + c * columns, width), columns)
        here = pl.ds(c * columns, columns)
        copies.append(
            (
                pltpu.make_async_copy(emb_hbm.at[:, pl.ds(there, columns)], emb.at[:, here], sems.at[0, c]),
                pltpu.make_async_copy(test_hbm.at[pl.ds(there, columns)], test.at[here], sems.at[1, c]),
            )
        )
    for pair in copies:
        for copy in pair:
            copy.start()
    sketch = jnp.zeros((rows, LANES), F32)
    for c in range(CHUNKS):
        for copy in copies[c]:
            copy.wait()
        here = slice(c * columns, (c + 1) * columns)
        parts = split(emb[:, here])
        terms, first = (keep_terms, 0) if c < CHUNKS // 2 else (send_terms, width // 2)
        for t in range(3):
            terms[t, :, here.start - first : here.stop - first] = parts[t]
            sketch += dot(parts[t], test[here])
    sketch_ref[...] = sketch
    left = split(sketch.T)
    for start in range(0, width // 2, STEP):
        image_blocks(left, [send_terms[t, :, start : start + STEP] for t in range(3)], send_ref, start // LANES)


def keep_kernel(sketch_ref, keep_terms, keep_ref):
    left = split(sketch_ref[...].T)
    for start in range(0, keep_terms.shape[2], STEP):
        image_blocks(left, [keep_terms[t, :, start : start + STEP] for t in range(3)], keep_ref, start // LANES)


def local_sketch(core, embeddings, test_matrix):
    rows, width = embeddings.shape
    half = width // 2
    vmem = pl.BlockSpec(memory_space=pltpu.VMEM)
    return pl.pallas_call(
        sketch_kernel,
        out_shape=[
            pltpu.VMEM((rows, LANES), F32),
            pltpu.VMEM((half // LANES, LANES, LANES), F32),
            pltpu.VMEM((3, rows, half), BF16),
        ],
        in_specs=[
            pl.BlockSpec(memory_space=pltpu.SMEM),
            pl.BlockSpec(memory_space=pltpu.HBM),
            pl.BlockSpec(memory_space=pltpu.HBM),
        ],
        out_specs=[vmem] * 3,
        scratch_shapes=[
            pltpu.VMEM((rows, width), F32),
            pltpu.VMEM((width, LANES), BF16),
            pltpu.VMEM((3, rows, half), BF16),
            pltpu.SemaphoreType.DMA((2, CHUNKS)),
        ],
        compiler_params=pltpu.CompilerParams(vmem_limit_bytes=VMEM_LIMIT),
        cost_estimate=pl.CostEstimate(flops=12 * rows * width * LANES, bytes_accessed=4 * rows * width, transcendentals=0),
        name="local_sketch",
    )(
        core,
        pltpu.with_memory_space_constraint(embeddings, pltpu.HBM),
        pltpu.with_memory_space_constraint(test_matrix, pltpu.HBM),
    )


def keep_image(sketch, keep_terms):
    rows, half = keep_terms.shape[1:]
    vmem = pl.BlockSpec(memory_space=pltpu.VMEM)
    return pl.pallas_call(
        keep_kernel,
        out_shape=pltpu.VMEM((half // LANES, LANES, LANES), F32),
        in_specs=[vmem] * 2,
        out_specs=vmem,
        compiler_params=pltpu.CompilerParams(vmem_limit_bytes=VMEM_LIMIT),
        cost_estimate=pl.CostEstimate(flops=12 * rows * half * LANES, bytes_accessed=6 * rows * half, transcendentals=0),
        name="keep_image",
    )(sketch, keep_terms)


def over_sublanes(tile, row):
    return jnp.broadcast_to(tile[row : row + 1], tile.shape)


def over_lanes(tile, lane):
    return jnp.broadcast_to(tile[:, lane : lane + 1], tile.shape)


def eliminate(a, b, first_lane):
    sublane = lax.broadcasted_iota(jnp.int32, (8, LANES), 0)
    tiles = range(len(a))
    column = {q: [over_lanes(a[q], first_lane + k) for k in range(8)] for q in tiles}
    for g in tiles:
        if g + 1 < len(a):
            for q in tiles[g:]:
                column[q] = column[q] + [over_lanes(a[q], first_lane + 8 * g + k) for k in range(8, 16)]
        for i in range(8):
            pivots = [over_sublanes(values, i) for values in column[g]]
            inverse = 1.0 / pivots[i]
            row_a, row_b = over_sublanes(a[g], i), over_sublanes(b[g], i)
            for q in tiles[g:]:
                factor = column[q][i] * inverse
                for k in range(i + 1, len(pivots)):
                    column[q][k] = column[q][k] - factor * pivots[k]
                if q == g:
                    factor = jnp.where(sublane > i, factor, 0.0)
                a[q] = a[q] - factor * row_a
                b[q] = b[q] - factor * row_b
        column = {q: column[q][8:] for q in tiles[g + 1 :]}


def factorize(gram):
    size = gram.shape[0]
    tiles = lambda value: [value[8 * t : 8 * t + 8] for t in range(PANEL // 8)]
    row = lax.broadcasted_iota(jnp.int32, (size, size), 0)
    column = lax.broadcasted_iota(jnp.int32, (size, size), 1)
    other = jnp.where(row == column, 1.0, 0.0).astype(F32)
    uppers, inverses = [], []
    for start in range(0, size, PANEL):
        a, b = tiles(gram), tiles(other)
        eliminate(a, b, start)
        a, b = jnp.concatenate(a, axis=0), jnp.concatenate(b, axis=0)
        here = row[start : start + PANEL]
        lanes = column[start : start + PANEL]
        scale = lax.rsqrt(jnp.sum(jnp.where(here == lanes, a, 0.0), axis=1, keepdims=True))
        upper, inverse = jnp.where(lanes >= here, a * scale, 0.0), b * scale
        uppers.append(upper)
        inverses.append(inverse)
        if start + PANEL < size:
            below = split(upper.T[start + PANEL :])
            change = dot_split(below, split(jnp.concatenate([upper, inverse], axis=1)))
            gram, other = gram[PANEL:] - change[:, :size], other[PANEL:] - change[:, size:]
    return jnp.concatenate(uppers, axis=0), jnp.concatenate(inverses, axis=0)


def finish_kernel(
    total_rows, place_ref, mine_ref, other_ref, sketch_ref, test_ref,
    basis_ref, right_ref, factor_ref, loadings, turned,
):
    blocks = mine_ref.shape[0]
    group = 16
    core = place_ref[0]
    halves = ((mine_ref, core), (other_ref, 1 - core))

    def wide(ref, first):
        return jnp.concatenate([ref[first + b] for b in range(group)], axis=1)

    partial = []
    for ref, half in halves:
        total = jnp.zeros((LANES, LANES), F32)
        for first in range(0, blocks, group):
            terms = split(wide(ref, first))
            offset = pl.multiple_of((half * blocks + first) * LANES, group * LANES)
            test = test_ref[pl.ds(offset, group * LANES), :]
            total += dot(terms[0], test) + (dot(terms[1], test) + dot(terms[2], test))
        partial.append(total)
    gram = (partial[0] + partial[1]) * (0.5 / total_rows)
    _, inverse = factorize(gram + gram.T)
    left = split(inverse)

    partial = []
    for h, (ref, _) in enumerate(halves):
        total, cross, small = (jnp.zeros((LANES, LANES), F32) for _ in range(3))
        for first in range(0, blocks, group):
            values = dot_split(left, split(wide(ref, first)))
            for b in range(group):
                loadings[h * blocks + first + b] = values[:, b * LANES : (b + 1) * LANES]
            terms = split(values)
            total += dot(terms[0], terms[0], 1)
            cross += dot(terms[1], terms[0], 1) + dot(terms[2], terms[0], 1)
            small += dot(terms[1], terms[1], 1)
        partial.append(total + (cross + cross.T + small))
    upper, second = factorize((partial[0] + partial[1]) / (2 * blocks * LANES))
    factor_ref[...] = upper.T

    basis_ref[...] = dot_split(split(sketch_ref[...]), left, 1)
    turned[...] = dot_split(split(second), split(loadings[place_ref[1]])).T
    right_ref[...] = turned[pl.ds(pl.multiple_of(place_ref[2], 8), right_ref.shape[0]), :]


def finish(place, mine, other, sketch, test_matrix, total_rows, own_rows):
    vmem = pl.BlockSpec(memory_space=pltpu.VMEM)
    return pl.pallas_call(
        functools.partial(finish_kernel, total_rows),
        out_shape=[
            jax.ShapeDtypeStruct(sketch.shape, F32),
            jax.ShapeDtypeStruct((own_rows, LANES), F32),
            jax.ShapeDtypeStruct((LANES, LANES), F32),
        ],
        in_specs=[pl.BlockSpec(memory_space=pltpu.SMEM)] + [vmem] * 4,
        out_specs=[vmem] * 3,
        scratch_shapes=[
            pltpu.VMEM((2 * mine.shape[0], LANES, LANES), F32),
            pltpu.VMEM((LANES, LANES), F32),
        ],
        compiler_params=pltpu.CompilerParams(vmem_limit_bytes=VMEM_LIMIT),
        name="finish",
    )(place, mine, other, sketch, test_matrix)


def exchange(values, axes):
    return lax.all_to_all(values, axes, 0, 0, tiled=False)


def scatter_sum(values, axes):
    parts = lax.axis_size(axes)
    blocks = values.reshape((parts, values.shape[0] // parts) + values.shape[1:])
    return jnp.sum(exchange(blocks, axes), axis=0)


def copies(values, axes):
    return exchange(jnp.broadcast_to(values[None], (lax.axis_size(axes),) + values.shape), axes)


def swap_cores(values):
    return lax.ppermute(values, "core", [(0, 1), (1, 0)])


def per_device(embeddings, test_matrix):
    devices_all = lax.axis_size(AXES)
    rows, width = embeddings.shape
    own_rows = width // devices_all
    core = lax.axis_index("core")
    sketch, send, keep_terms = local_sketch(core.reshape(1), embeddings, test_matrix)
    arriving = swap_cores(send)
    image = keep_image(sketch, keep_terms) + arriving
    piece = scatter_sum(image.reshape(-1, LANES), NEAR)
    piece = jnp.sum(copies(piece, "z_pair"), axis=0)
    mine = copies(piece, NEAR).reshape(image.shape)
    other = swap_cores(mine)
    first = lax.axis_index(AXES) * own_rows
    half_blocks = mine.shape[0]
    own_block = first // LANES
    slot = jnp.where(own_block // half_blocks == core, 0, half_blocks) + own_block % half_blocks
    place = jnp.stack([core, slot, first % LANES])
    basis, right_basis, factor = finish(place, mine, other, sketch, test_matrix, rows * devices_all, own_rows)
    return (basis, right_basis, factor)


def solution(mesh):
    fine = Mesh(mesh.devices.reshape(4, 8, 2, 2, 4), AXES)
    return jax.shard_map(
        per_device,
        mesh=fine,
        in_specs=(P(AXES, None), P()),
        out_specs=(P(AXES, None), P(AXES, None), P()),
        check_vma=False,
    )
```

```python
import functools

import jax
import jax.numpy as jnp
from jax import lax
from jax.experimental import pallas as pl
from jax.experimental.pallas import tpu as pltpu
from jax.sharding import Mesh, PartitionSpec as P

AXES = ("y", "z_pair", "z_in_pair", "core", "x")
NEAR = ("x", "y", "z_in_pair")
CHUNKS = 4
STEP = 512
PANEL = 32
SPREAD = 2.0
LANES = 128
F32, BF16 = jnp.float32, jnp.bfloat16
VMEM_LIMIT = 24 * 1024 * 1024


def dot(left, right, right_dim=0):
    return lax.dot_general(left, right, (((1,), (right_dim,)), ((), ())), preferred_element_type=F32)


def split(values):
    first = values.astype(BF16)
    rest = values - first.astype(F32)
    second = rest.astype(BF16)
    return first, second, (rest - second.astype(F32)).astype(BF16)


def dot_split(left, right, right_dim=0):
    return dot(left[0], right[0], right_dim) + (
        (dot(left[1], right[0], right_dim) + dot(left[0], right[1], right_dim))
        + (dot(left[2], right[0], right_dim) + dot(left[1], right[1], right_dim) + dot(left[0], right[2], right_dim))
    )


def image_blocks(left, right, out, first):
    part = dot(left[0], right[0]) + (
        (dot(left[1], right[0]) + dot(left[0], right[1]))
        + (dot(left[2], right[0]) + dot(left[1], right[1]) + dot(left[0], right[2]))
    )
    for b in range(part.shape[1] // LANES):
        out[first + b] = part[:, b * LANES : (b + 1) * LANES]


def sketch_kernel(core_ref, emb_hbm, test_hbm, sketch_ref, send_ref, keep_terms, emb, test, send_terms, sems):
    rows, width = emb.shape
    columns = width // CHUNKS
    core = core_ref[0]
    copies = []
    for c in range(CHUNKS):
        there = pl.multiple_of(lax.rem(core * (width // 2) + c * columns, width), columns)
        here = pl.ds(c * columns, columns)
        copies.append(
            (
                pltpu.make_async_copy(emb_hbm.at[:, pl.ds(there, columns)], emb.at[:, here], sems.at[0, c]),
                pltpu.make_async_copy(test_hbm.at[pl.ds(there, columns)], test.at[here], sems.at[1, c]),
            )
        )
    for pair in copies:
        for copy in pair:
            copy.start()
    sketch = jnp.zeros((rows, LANES), F32)
    for c in range(CHUNKS):
        for copy in copies[c]:
            copy.wait()
        here = slice(c * columns, (c + 1) * columns)
        parts = split(emb[:, here])
        terms, first = (keep_terms, 0) if c < CHUNKS // 2 else (send_terms, width // 2)
        for t in range(3):
            terms[t, :, here.start - first : here.stop - first] = parts[t]
            sketch += dot(parts[t], test[here])
    sketch_ref[...] = sketch
    left = split(sketch.T)
    for start in range(0, width // 2, STEP):
        image_blocks(left, [send_terms[t, :, start : start + STEP] for t in range(3)], send_ref, start // LANES)


def keep_kernel(sketch_ref, keep_terms, keep_ref):
    left = split(sketch_ref[...].T)
    for start in range(0, keep_terms.shape[2], STEP):
        image_blocks(left, [keep_terms[t, :, start : start + STEP] for t in range(3)], keep_ref, start // LANES)


def local_sketch(core, embeddings, test_matrix):
    rows, width = embeddings.shape
    half = width // 2
    vmem = pl.BlockSpec(memory_space=pltpu.VMEM)
    return pl.pallas_call(
        sketch_kernel,
        out_shape=[
            pltpu.VMEM((rows, LANES), F32),
            pltpu.VMEM((half // LANES, LANES, LANES), F32),
            pltpu.VMEM((3, rows, half), BF16),
        ],
        in_specs=[
            pl.BlockSpec(memory_space=pltpu.SMEM),
            pl.BlockSpec(memory_space=pltpu.HBM),
            pl.BlockSpec(memory_space=pltpu.HBM),
        ],
        out_specs=[vmem] * 3,
        scratch_shapes=[
            pltpu.VMEM((rows, width), F32),
            pltpu.VMEM((width, LANES), BF16),
            pltpu.VMEM((3, rows, half), BF16),
            pltpu.SemaphoreType.DMA((2, CHUNKS)),
        ],
        compiler_params=pltpu.CompilerParams(vmem_limit_bytes=VMEM_LIMIT),
        cost_estimate=pl.CostEstimate(flops=12 * rows * width * LANES, bytes_accessed=4 * rows * width, transcendentals=0),
        name="local_sketch",
    )(
        core,
        pltpu.with_memory_space_constraint(embeddings, pltpu.HBM),
        pltpu.with_memory_space_constraint(test_matrix, pltpu.HBM),
    )


def keep_image(sketch, keep_terms):
    rows, half = keep_terms.shape[1:]
    vmem = pl.BlockSpec(memory_space=pltpu.VMEM)
    return pl.pallas_call(
        keep_kernel,
        out_shape=pltpu.VMEM((half // LANES, LANES, LANES), F32),
        in_specs=[vmem] * 2,
        out_specs=vmem,
        compiler_params=pltpu.CompilerParams(vmem_limit_bytes=VMEM_LIMIT),
        cost_estimate=pl.CostEstimate(flops=12 * rows * half * LANES, bytes_accessed=6 * rows * half, transcendentals=0),
        name="keep_image",
    )(sketch, keep_terms)


def over_sublanes(tile, row):
    return jnp.broadcast_to(tile[row : row + 1], tile.shape)


def over_lanes(tile, lane):
    return jnp.broadcast_to(tile[:, lane : lane + 1], tile.shape)


def eliminate(a, b, first_lane):
    sublane = lax.broadcasted_iota(jnp.int32, (8, LANES), 0)
    tiles = range(len(a))
    column = {q: [over_lanes(a[q], first_lane + k) for k in range(8)] for q in tiles}
    for g in tiles:
        if g + 1 < len(a):
            for q in tiles[g:]:
                column[q] = column[q] + [over_lanes(a[q], first_lane + 8 * g + k) for k in range(8, 16)]
        for i in range(8):
            pivots = [over_sublanes(values, i) for values in column[g]]
            inverse = 1.0 / pivots[i]
            row_a, row_b = over_sublanes(a[g], i), over_sublanes(b[g], i)
            for q in tiles[g:]:
                factor = column[q][i] * inverse
                for k in range(i + 1, len(pivots)):
                    column[q][k] = column[q][k] - factor * pivots[k]
                if q == g:
                    factor = jnp.where(sublane > i, factor, 0.0)
                a[q] = a[q] - factor * row_a
                b[q] = b[q] - factor * row_b
            yield
        column = {q: column[q][8:] for q in tiles[g + 1 :]}


def factor_steps(gram, result):
    size = gram.shape[0]
    tiles = lambda value: [value[8 * t : 8 * t + 8] for t in range(PANEL // 8)]
    row = lax.broadcasted_iota(jnp.int32, (size, size), 0)
    column = lax.broadcasted_iota(jnp.int32, (size, size), 1)
    other = jnp.where(row == column, 1.0, 0.0).astype(F32)
    uppers, inverses = [], []
    for start in range(0, size, PANEL):
        a, b = tiles(gram), tiles(other)
        yield from eliminate(a, b, start)
        a, b = jnp.concatenate(a, axis=0), jnp.concatenate(b, axis=0)
        here = row[start : start + PANEL]
        lanes = column[start : start + PANEL]
        scale = lax.rsqrt(jnp.sum(jnp.where(here == lanes, a, 0.0), axis=1, keepdims=True))
        upper, inverse = jnp.where(lanes >= here, a * scale, 0.0), b * scale
        uppers.append(upper)
        inverses.append(inverse)
        yield
        if start + PANEL < size:
            below = split(upper.T[start + PANEL :])
            change = dot_split(below, split(jnp.concatenate([upper, inverse], axis=1)))
            gram, other = gram[PANEL:] - change[:, :size], other[PANEL:] - change[:, size:]
        yield
    result += [jnp.concatenate(uppers, axis=0), jnp.concatenate(inverses, axis=0)]


def factorize(*grams):
    results = [[] for _ in grams]
    for _ in zip(*(factor_steps(gram, result) for gram, result in zip(grams, results, strict=True)), strict=True):
        pass
    return results


def self_products(terms):
    cross = dot(terms[1], terms[0], 1) + dot(terms[2], terms[0], 1)
    return dot(terms[0], terms[0], 1) + (cross + cross.T + dot(terms[1], terms[1], 1))


def finish_kernel(
    total_rows, place_ref, mine_ref, other_ref, sketch_ref, test_ref,
    basis_ref, right_ref, factor_ref, loadings, inverse_first, turned,
):
    blocks = mine_ref.shape[0]
    width = 2 * blocks * LANES
    core = place_ref[0]

    def wide(ref):
        return jnp.concatenate([ref[b] for b in range(blocks)], axis=1)

    def write_right(inverse, block):
        turned[...] = dot_split(split(inverse), split(block)).T
        right_ref[...] = turned[pl.ds(pl.multiple_of(place_ref[2], 8), right_ref.shape[0]), :]

    sketch_parts, image_parts = [], []
    for ref, half in ((mine_ref, core), (other_ref, 1 - core)):
        terms = split(wide(ref))
        test = test_ref[pl.ds(pl.multiple_of(half * blocks * LANES, blocks * LANES), blocks * LANES), :]
        sketch_parts.append(dot(terms[0], test) + (dot(terms[1], test) + dot(terms[2], test)))
        image_parts.append(self_products(terms))
    gram = (sketch_parts[0] + sketch_parts[1]) * (0.5 / total_rows)
    image_gram = (image_parts[0] + image_parts[1]) * (1.0 / width)
    (_, inverse), (upper_image, inverse_image) = factorize(gram + gram.T, image_gram)
    left = split(inverse)
    inverse_first[...] = inverse
    basis_ref[...] = dot_split(split(sketch_ref[...]), left, 1)
    factor_ref[...] = dot_split(left, split(upper_image), 1)
    slot = lax.rem(place_ref[1], blocks)
    write_right(inverse_image, jnp.where(place_ref[1] < blocks, mine_ref[slot], other_ref[slot]))

    row = lax.broadcasted_iota(jnp.int32, (LANES, LANES), 0)
    column = lax.broadcasted_iota(jnp.int32, (LANES, LANES), 1)
    trace = jnp.sum(jnp.where(row == column, image_gram, 0.0))
    spread = trace * jnp.sum(inverse_image * inverse_image)

    @pl.when(jnp.logical_not(spread <= SPREAD * LANES * LANES))
    def _():
        left = split(inverse_first[...])
        pair = jnp.concatenate([left[0], left[1]], axis=1)
        parts = []
        for h, ref in enumerate((mine_ref, other_ref)):
            x = split(wide(ref))
            values = dot(pair, jnp.concatenate([x[0], x[0]], axis=0)) + (
                dot(pair, jnp.concatenate([x[1], x[1]], axis=0))
                + dot(jnp.concatenate([left[2], left[0]], axis=1), jnp.concatenate([x[0], x[2]], axis=0))
            )
            for b in range(blocks):
                loadings[h * blocks + b] = values[:, b * LANES : (b + 1) * LANES]
            parts.append(self_products(split(values)))
        ((upper, second),) = factorize((parts[0] + parts[1]) * (1.0 / width))
        factor_ref[...] = upper.T
        write_right(second, loadings[place_ref[1]])


def finish(place, mine, other, sketch, test_matrix, total_rows, own_rows):
    vmem = pl.BlockSpec(memory_space=pltpu.VMEM)
    return pl.pallas_call(
        functools.partial(finish_kernel, total_rows),
        out_shape=[
            jax.ShapeDtypeStruct(sketch.shape, F32),
            jax.ShapeDtypeStruct((own_rows, LANES), F32),
            jax.ShapeDtypeStruct((LANES, LANES), F32),
        ],
        in_specs=[pl.BlockSpec(memory_space=pltpu.SMEM)] + [vmem] * 4,
        out_specs=[vmem] * 3,
        scratch_shapes=[
            pltpu.VMEM((2 * mine.shape[0], LANES, LANES), F32),
            pltpu.VMEM((LANES, LANES), F32),
            pltpu.VMEM((LANES, LANES), F32),
        ],
        compiler_params=pltpu.CompilerParams(vmem_limit_bytes=VMEM_LIMIT),
        name="finish",
    )(place, mine, other, sketch, test_matrix)


def exchange(values, axes):
    return lax.all_to_all(values, axes, 0, 0, tiled=False)


def scatter_sum(values, axes):
    parts = lax.axis_size(axes)
    blocks = values.reshape((parts, values.shape[0] // parts) + values.shape[1:])
    return jnp.sum(exchange(blocks, axes), axis=0)


def copies(values, axes):
    return exchange(jnp.broadcast_to(values[None], (lax.axis_size(axes),) + values.shape), axes)


def swap_cores(values):
    return lax.ppermute(values, "core", [(0, 1), (1, 0)])


def per_device(embeddings, test_matrix):
    devices_all = lax.axis_size(AXES)
    rows, width = embeddings.shape
    own_rows = width // devices_all
    core = lax.axis_index("core")
    sketch, send, keep_terms = local_sketch(core.reshape(1), embeddings, test_matrix)
    arriving = swap_cores(send)
    image = keep_image(sketch, keep_terms) + arriving
    piece = scatter_sum(image.reshape(-1, LANES), NEAR)
    piece = jnp.sum(copies(piece, "z_pair"), axis=0)
    mine = copies(piece, NEAR).reshape(image.shape)
    other = swap_cores(mine)
    first = lax.axis_index(AXES) * own_rows
    half_blocks = mine.shape[0]
    own_block = first // LANES
    slot = jnp.where(own_block // half_blocks == core, 0, half_blocks) + own_block % half_blocks
    place = jnp.stack([core, slot, first % LANES])
    basis, right_basis, factor = finish(place, mine, other, sketch, test_matrix, rows * devices_all, own_rows)
    return (basis, right_basis, factor)


def solution(mesh):
    fine = Mesh(mesh.devices.reshape(4, 8, 2, 2, 4), AXES)
    return jax.shard_map(
        per_device,
        mesh=fine,
        in_specs=(P(AXES, None), P()),
        out_specs=(P(AXES, None), P(AXES, None), P()),
        check_vma=False,
    )
```

```python
import functools

import jax
import jax.numpy as jnp
from jax import lax
from jax.experimental import pallas as pl
from jax.experimental.pallas import tpu as pltpu
from jax.sharding import Mesh, PartitionSpec as P

AXES = ("y", "z_pair", "z_in_pair", "core", "x")
NEAR = ("x", "y", "z_in_pair")
CHUNKS = 4
STEP = 2048
PANEL = 32
SPREAD = 2.0
LANES = 128
F32, BF16 = jnp.float32, jnp.bfloat16
VMEM_LIMIT = 24 * 1024 * 1024


def dot(left, right, right_dim=0):
    return lax.dot_general(left, right, (((1,), (right_dim,)), ((), ())), preferred_element_type=F32)


def split(values):
    first = values.astype(BF16)
    rest = values - first.astype(F32)
    second = rest.astype(BF16)
    return first, second, (rest - second.astype(F32)).astype(BF16)


def dot_split(left, right, right_dim=0):
    return dot(left[0], right[0], right_dim) + (
        (dot(left[1], right[0], right_dim) + dot(left[0], right[1], right_dim))
        + (dot(left[2], right[0], right_dim) + dot(left[1], right[1], right_dim) + dot(left[0], right[2], right_dim))
    )


def image_blocks(left, right, out, first):
    part = dot(left[0], right[0]) + (
        (dot(left[1], right[0]) + dot(left[0], right[1]))
        + (dot(left[2], right[0]) + dot(left[1], right[1]) + dot(left[0], right[2]))
    )
    for b in range(part.shape[1] // LANES):
        out[first + b] = part[:, b * LANES : (b + 1) * LANES]


def sketch_kernel(core_ref, emb_hbm, test_hbm, sketch_ref, send_ref, keep_terms, emb, test, send_terms, sems):
    rows, width = emb.shape
    columns = width // CHUNKS
    core = core_ref[0]
    copies = []
    for c in range(CHUNKS):
        there = pl.multiple_of(lax.rem(core * (width // 2) + c * columns, width), columns)
        here = pl.ds(c * columns, columns)
        copies.append(
            (
                pltpu.make_async_copy(emb_hbm.at[:, pl.ds(there, columns)], emb.at[:, here], sems.at[0, c]),
                pltpu.make_async_copy(test_hbm.at[pl.ds(there, columns)], test.at[here], sems.at[1, c]),
            )
        )
    for pair in copies:
        for copy in pair:
            copy.start()
    sketch = jnp.zeros((rows, LANES), F32)
    for c in range(CHUNKS):
        for copy in copies[c]:
            copy.wait()
        here = slice(c * columns, (c + 1) * columns)
        parts = split(emb[:, here])
        terms, first = (keep_terms, 0) if c < CHUNKS // 2 else (send_terms, width // 2)
        for t in range(3):
            terms[t, :, here.start - first : here.stop - first] = parts[t]
            sketch += dot(parts[t], test[here])
    sketch_ref[...] = sketch
    left = split(sketch.T)
    for start in range(0, width // 2, STEP):
        image_blocks(left, [send_terms[t, :, start : start + STEP] for t in range(3)], send_ref, start // LANES)


def keep_kernel(sketch_ref, keep_terms, keep_ref):
    left = split(sketch_ref[...].T)
    for start in range(0, keep_terms.shape[2], STEP):
        image_blocks(left, [keep_terms[t, :, start : start + STEP] for t in range(3)], keep_ref, start // LANES)


def local_sketch(core, embeddings, test_matrix):
    rows, width = embeddings.shape
    half = width // 2
    vmem = pl.BlockSpec(memory_space=pltpu.VMEM)
    return pl.pallas_call(
        sketch_kernel,
        out_shape=[
            pltpu.VMEM((rows, LANES), F32),
            pltpu.VMEM((half // LANES, LANES, LANES), F32),
            pltpu.VMEM((3, rows, half), BF16),
        ],
        in_specs=[
            pl.BlockSpec(memory_space=pltpu.SMEM),
            pl.BlockSpec(memory_space=pltpu.HBM),
            pl.BlockSpec(memory_space=pltpu.HBM),
        ],
        out_specs=[vmem] * 3,
        scratch_shapes=[
            pltpu.VMEM((rows, width), F32),
            pltpu.VMEM((width, LANES), BF16),
            pltpu.VMEM((3, rows, half), BF16),
            pltpu.SemaphoreType.DMA((2, CHUNKS)),
        ],
        compiler_params=pltpu.CompilerParams(vmem_limit_bytes=VMEM_LIMIT),
        cost_estimate=pl.CostEstimate(flops=12 * rows * width * LANES, bytes_accessed=4 * rows * width, transcendentals=0),
        name="local_sketch",
    )(
        core,
        pltpu.with_memory_space_constraint(embeddings, pltpu.HBM),
        pltpu.with_memory_space_constraint(test_matrix, pltpu.HBM),
    )


def keep_image(sketch, keep_terms):
    rows, half = keep_terms.shape[1:]
    vmem = pl.BlockSpec(memory_space=pltpu.VMEM)
    return pl.pallas_call(
        keep_kernel,
        out_shape=pltpu.VMEM((half // LANES, LANES, LANES), F32),
        in_specs=[vmem] * 2,
        out_specs=vmem,
        compiler_params=pltpu.CompilerParams(vmem_limit_bytes=VMEM_LIMIT),
        cost_estimate=pl.CostEstimate(flops=12 * rows * half * LANES, bytes_accessed=6 * rows * half, transcendentals=0),
        name="keep_image",
    )(sketch, keep_terms)


def over_sublanes(tile, row):
    return jnp.broadcast_to(tile[row : row + 1], tile.shape)


def over_lanes(tile, lane):
    return jnp.broadcast_to(tile[:, lane : lane + 1], tile.shape)


def eliminate(a, b, first_lane):
    sublane = lax.broadcasted_iota(jnp.int32, (8, LANES), 0)
    spread = lambda tile, first: [over_lanes(tile, first + k) for k in range(8)]
    last = len(a) - 1
    ahead = spread(a[0], first_lane)
    for g in range(last + 1):
        first = first_lane + 8 * g
        column = {q: spread(a[q], first) for q in range(g + 1, last + 1)}
        column[g] = ahead
        if g < last:
            column[g] = column[g] + spread(a[g], first + 8)
            column[g + 1] = column[g + 1] + spread(a[g + 1], first + 8)
        for i in range(8):
            pivots = [over_sublanes(values, i) for values in column[g]]
            inverse = 1.0 / pivots[i]
            row_a, row_b = over_sublanes(a[g], i), over_sublanes(b[g], i)
            for q in range(g, last + 1):
                factor = column[q][i] * inverse
                for k in range(i + 1, len(column[q])):
                    column[q][k] = column[q][k] - factor * pivots[k]
                if q == g:
                    factor = jnp.where(sublane > i, factor, 0.0)
                a[q] = a[q] - factor * row_a
                b[q] = b[q] - factor * row_b
            yield
        if g < last:
            ahead = column[g + 1][8:]


def factor_steps(gram, result):
    size = gram.shape[0]
    tiles = lambda value: [value[8 * t : 8 * t + 8] for t in range(PANEL // 8)]
    row = lax.broadcasted_iota(jnp.int32, (size, size), 0)
    column = lax.broadcasted_iota(jnp.int32, (size, size), 1)
    other = jnp.where(row == column, 1.0, 0.0).astype(F32)
    uppers, inverses = [], []
    for start in range(0, size, PANEL):
        a, b = tiles(gram), tiles(other)
        yield from eliminate(a, b, start)
        a, b = jnp.concatenate(a, axis=0), jnp.concatenate(b, axis=0)
        here = row[start : start + PANEL]
        lanes = column[start : start + PANEL]
        scale = lax.rsqrt(jnp.sum(jnp.where(here == lanes, a, 0.0), axis=1, keepdims=True))
        upper, inverse = jnp.where(lanes >= here, a * scale, 0.0), b * scale
        uppers.append(upper)
        inverses.append(inverse)
        yield
        if start + PANEL < size:
            below = split(upper.T[start + PANEL :])
            change = dot_split(below, split(jnp.concatenate([upper, inverse], axis=1)))
            gram, other = gram[PANEL:] - change[:, :size], other[PANEL:] - change[:, size:]
        yield
    result += [jnp.concatenate(uppers, axis=0), jnp.concatenate(inverses, axis=0)]


def factorize(*grams):
    results = [[] for _ in grams]
    for _ in zip(*(factor_steps(gram, result) for gram, result in zip(grams, results, strict=True)), strict=True):
        pass
    return results


def self_products(terms):
    cross = dot(terms[1], terms[0], 1) + dot(terms[2], terms[0], 1)
    return dot(terms[0], terms[0], 1) + (cross + cross.T + dot(terms[1], terms[1], 1))


def grams_kernel(half_ref, ref, test_ref, grams_ref):
    columns = ref.shape[0] * LANES
    terms = split(jnp.concatenate([ref[b] for b in range(ref.shape[0])], axis=1))
    test = test_ref[pl.ds(pl.multiple_of(half_ref[0] * columns, columns), columns), :]
    grams_ref[0] = dot(terms[0], test) + (dot(terms[1], test) + dot(terms[2], test))
    grams_ref[1] = self_products(terms)


def half_grams(half, image, test_matrix):
    vmem = pl.BlockSpec(memory_space=pltpu.VMEM)
    return pl.pallas_call(
        grams_kernel,
        out_shape=pltpu.VMEM((2, LANES, LANES), F32),
        in_specs=[pl.BlockSpec(memory_space=pltpu.SMEM), vmem, vmem],
        out_specs=vmem,
        compiler_params=pltpu.CompilerParams(vmem_limit_bytes=VMEM_LIMIT),
        cost_estimate=pl.CostEstimate(flops=14 * LANES * image.size, bytes_accessed=4 * image.size, transcendentals=0),
        name="half_grams",
    )(half.reshape(1), image, test_matrix)


def finish_kernel(
    total_rows, place_ref, mine_grams, other_grams, mine_ref, other_ref, sketch_ref,
    basis_ref, right_ref, factor_ref, loadings, inverse_first, turned,
):
    blocks = mine_ref.shape[0]
    width = 2 * blocks * LANES
    core, own_block = place_ref[0], place_ref[1]

    def image_block(half, b):
        return jnp.where(core == half, mine_ref[b], other_ref[b])

    def write_right(inverse, block):
        turned[...] = dot_split(split(inverse), split(block)).T
        right_ref[...] = turned[pl.ds(pl.multiple_of(place_ref[2], 8), right_ref.shape[0]), :]

    gram = (mine_grams[0] + other_grams[0]) * (0.5 / total_rows)
    image_gram = (mine_grams[1] + other_grams[1]) * (1.0 / width)
    (_, inverse), (upper_image, inverse_image) = factorize(gram + gram.T, image_gram)
    left = split(inverse)
    inverse_first[...] = inverse
    basis_ref[...] = dot_split(split(sketch_ref[...]), left, 1)
    factor_ref[...] = dot_split(left, split(upper_image), 1)
    write_right(inverse_image, image_block(own_block // blocks, lax.rem(own_block, blocks)))

    row = lax.broadcasted_iota(jnp.int32, (LANES, LANES), 0)
    column = lax.broadcasted_iota(jnp.int32, (LANES, LANES), 1)
    trace = jnp.sum(jnp.where(row == column, image_gram, 0.0))
    spread = trace * jnp.sum(inverse_image * inverse_image)

    @pl.when(jnp.logical_not(spread <= SPREAD * LANES * LANES))
    def _():
        left = split(inverse_first[...])
        pair = jnp.concatenate([left[0], left[1]], axis=1)
        parts = []
        for half in range(2):
            x = split(jnp.concatenate([image_block(half, b) for b in range(blocks)], axis=1))
            values = dot(pair, jnp.concatenate([x[0], x[0]], axis=0)) + (
                dot(pair, jnp.concatenate([x[1], x[1]], axis=0))
                + dot(jnp.concatenate([left[2], left[0]], axis=1), jnp.concatenate([x[0], x[2]], axis=0))
            )
            for b in range(blocks):
                loadings[half * blocks + b] = values[:, b * LANES : (b + 1) * LANES]
            parts.append(self_products(split(values)))
        ((upper, second),) = factorize((parts[0] + parts[1]) * (1.0 / width))
        factor_ref[...] = upper.T
        write_right(second, loadings[own_block])


def finish(place, mine_grams, other_grams, mine, other, sketch, total_rows, own_rows):
    vmem = pl.BlockSpec(memory_space=pltpu.VMEM)
    return pl.pallas_call(
        functools.partial(finish_kernel, total_rows),
        out_shape=[
            jax.ShapeDtypeStruct(sketch.shape, F32),
            jax.ShapeDtypeStruct((own_rows, LANES), F32),
            jax.ShapeDtypeStruct((LANES, LANES), F32),
        ],
        in_specs=[pl.BlockSpec(memory_space=pltpu.SMEM)] + [vmem] * 5,
        out_specs=[vmem] * 3,
        scratch_shapes=[
            pltpu.VMEM((2 * mine.shape[0], LANES, LANES), F32),
            pltpu.VMEM((LANES, LANES), F32),
            pltpu.VMEM((LANES, LANES), F32),
        ],
        compiler_params=pltpu.CompilerParams(vmem_limit_bytes=VMEM_LIMIT),
        name="finish",
    )(place, mine_grams, other_grams, mine, other, sketch)


def exchange(values, axes):
    return lax.all_to_all(values, axes, 0, 0, tiled=False)


def scatter_sum(values, axes):
    parts = lax.axis_size(axes)
    blocks = values.reshape((parts, values.shape[0] // parts) + values.shape[1:])
    return jnp.sum(exchange(blocks, axes), axis=0)


def copies(values, axes):
    return exchange(jnp.broadcast_to(values[None], (lax.axis_size(axes),) + values.shape), axes)


def swap_cores(values):
    return lax.ppermute(values, "core", [(0, 1), (1, 0)])


def per_device(embeddings, test_matrix):
    devices_all = lax.axis_size(AXES)
    rows, width = embeddings.shape
    own_rows = width // devices_all
    core = lax.axis_index("core")
    sketch, send, keep_terms = local_sketch(core.reshape(1), embeddings, test_matrix)
    arriving = swap_cores(send)
    image = keep_image(sketch, keep_terms) + arriving
    piece = scatter_sum(image.reshape(-1, LANES), NEAR)
    piece = jnp.sum(copies(piece, "z_pair"), axis=0)
    mine = copies(piece, NEAR).reshape(image.shape)
    other = swap_cores(mine)
    mine_grams = half_grams(core, mine, test_matrix)
    other_grams = half_grams(1 - core, other, test_matrix)
    first = lax.axis_index(AXES) * own_rows
    place = jnp.stack([core, first // LANES, first % LANES])
    basis, right_basis, factor = finish(place, mine_grams, other_grams, mine, other, sketch, rows * devices_all, own_rows)
    return (basis, right_basis, factor)


def solution(mesh):
    fine = Mesh(mesh.devices.reshape(4, 8, 2, 2, 4), AXES)
    return jax.shard_map(
        per_device,
        mesh=fine,
        in_specs=(P(AXES, None), P()),
        out_specs=(P(AXES, None), P(AXES, None), P()),
        check_vma=False,
    )
```

```python
import functools

import jax
import jax.numpy as jnp
from jax import lax
from jax.experimental import pallas as pl
from jax.experimental.pallas import tpu as pltpu
from jax.sharding import Mesh, PartitionSpec as P

AXES = ("y", "z_pair", "z_in_pair", "core", "x")
NEAR = ("z_in_pair", "x", "y")
CHUNKS = 4
STEP = 2048
PANEL = 32
SPREAD = 2.0
LANES = 128
F32, BF16 = jnp.float32, jnp.bfloat16
VMEM_LIMIT = 24 * 1024 * 1024


def dot(left, right, right_dim=0):
    return lax.dot_general(left, right, (((1,), (right_dim,)), ((), ())), preferred_element_type=F32)


def split(values):
    first = values.astype(BF16)
    rest = values - first.astype(F32)
    second = rest.astype(BF16)
    return first, second, (rest - second.astype(F32)).astype(BF16)


def dot_split(left, right, right_dim=0):
    return dot(left[0], right[0], right_dim) + (
        (dot(left[1], right[0], right_dim) + dot(left[0], right[1], right_dim))
        + (dot(left[2], right[0], right_dim) + dot(left[1], right[1], right_dim) + dot(left[0], right[2], right_dim))
    )


def image_blocks(left, right, out, first):
    part = dot(left[0], right[0]) + (
        (dot(left[1], right[0]) + dot(left[0], right[1]))
        + (dot(left[2], right[0]) + dot(left[1], right[1]) + dot(left[0], right[2]))
    )
    for b in range(part.shape[1] // LANES):
        out[first + b] = part[:, b * LANES : (b + 1) * LANES]


def sketch_kernel(core_ref, emb_hbm, test_hbm, sketch_ref, send_ref, keep_terms, emb, test, send_terms, sems):
    rows, width = emb.shape
    columns = width // CHUNKS
    core = core_ref[0]
    copies = []
    for c in range(CHUNKS):
        there = pl.multiple_of(lax.rem(core * (width // 2) + c * columns, width), columns)
        here = pl.ds(c * columns, columns)
        copies.append(
            (
                pltpu.make_async_copy(emb_hbm.at[:, pl.ds(there, columns)], emb.at[:, here], sems.at[0, c]),
                pltpu.make_async_copy(test_hbm.at[pl.ds(there, columns)], test.at[here], sems.at[1, c]),
            )
        )
    for pair in copies:
        for copy in pair:
            copy.start()
    sketch = jnp.zeros((rows, LANES), F32)
    for c in range(CHUNKS):
        for copy in copies[c]:
            copy.wait()
        here = slice(c * columns, (c + 1) * columns)
        parts = split(emb[:, here])
        terms, first = (keep_terms, 0) if c < CHUNKS // 2 else (send_terms, width // 2)
        for t in range(3):
            terms[t, :, here.start - first : here.stop - first] = parts[t]
            sketch += dot(parts[t], test[here])
    sketch_ref[...] = sketch
    left = split(sketch.T)
    for start in range(0, width // 2, STEP):
        image_blocks(left, [send_terms[t, :, start : start + STEP] for t in range(3)], send_ref, start // LANES)


def keep_kernel(sketch_ref, keep_terms, keep_ref):
    left = split(sketch_ref[...].T)
    for start in range(0, keep_terms.shape[2], STEP):
        image_blocks(left, [keep_terms[t, :, start : start + STEP] for t in range(3)], keep_ref, start // LANES)


def local_sketch(core, embeddings, test_matrix):
    rows, width = embeddings.shape
    half = width // 2
    vmem = pl.BlockSpec(memory_space=pltpu.VMEM)
    return pl.pallas_call(
        sketch_kernel,
        out_shape=[
            pltpu.VMEM((rows, LANES), F32),
            pltpu.VMEM((half // LANES, LANES, LANES), F32),
            pltpu.VMEM((3, rows, half), BF16),
        ],
        in_specs=[
            pl.BlockSpec(memory_space=pltpu.SMEM),
            pl.BlockSpec(memory_space=pltpu.HBM),
            pl.BlockSpec(memory_space=pltpu.HBM),
        ],
        out_specs=[vmem] * 3,
        scratch_shapes=[
            pltpu.VMEM((rows, width), F32),
            pltpu.VMEM((width, LANES), BF16),
            pltpu.VMEM((3, rows, half), BF16),
            pltpu.SemaphoreType.DMA((2, CHUNKS)),
        ],
        compiler_params=pltpu.CompilerParams(vmem_limit_bytes=VMEM_LIMIT),
        cost_estimate=pl.CostEstimate(flops=12 * rows * width * LANES, bytes_accessed=4 * rows * width, transcendentals=0),
        name="local_sketch",
    )(
        core,
        pltpu.with_memory_space_constraint(embeddings, pltpu.HBM),
        pltpu.with_memory_space_constraint(test_matrix, pltpu.HBM),
    )


def keep_image(sketch, keep_terms):
    rows, half = keep_terms.shape[1:]
    vmem = pl.BlockSpec(memory_space=pltpu.VMEM)
    return pl.pallas_call(
        keep_kernel,
        out_shape=pltpu.VMEM((half // LANES, LANES, LANES), F32),
        in_specs=[vmem] * 2,
        out_specs=vmem,
        compiler_params=pltpu.CompilerParams(vmem_limit_bytes=VMEM_LIMIT),
        cost_estimate=pl.CostEstimate(flops=12 * rows * half * LANES, bytes_accessed=6 * rows * half, transcendentals=0),
        name="keep_image",
    )(sketch, keep_terms)


def over_sublanes(tile, row):
    return jnp.broadcast_to(tile[row : row + 1], tile.shape)


def over_lanes(tile, lane):
    return jnp.broadcast_to(tile[:, lane : lane + 1], tile.shape)


def eliminate(a, b, first_lane):
    sublane = lax.broadcasted_iota(jnp.int32, (8, LANES), 0)
    spread = lambda tile, first: [over_lanes(tile, first + k) for k in range(8)]
    last = len(a) - 1
    ahead = spread(a[0], first_lane)
    for g in range(last + 1):
        first = first_lane + 8 * g
        column = {q: spread(a[q], first) for q in range(g + 1, last + 1)}
        column[g] = ahead
        if g < last:
            column[g] = column[g] + spread(a[g], first + 8)
            column[g + 1] = column[g + 1] + spread(a[g + 1], first + 8)
        for i in range(8):
            pivots = [over_sublanes(values, i) for values in column[g]]
            inverse = 1.0 / pivots[i]
            row_a, row_b = over_sublanes(a[g], i), over_sublanes(b[g], i)
            for q in range(g, last + 1):
                factor = column[q][i] * inverse
                for k in range(i + 1, len(column[q])):
                    column[q][k] = column[q][k] - factor * pivots[k]
                if q == g:
                    factor = jnp.where(sublane > i, factor, 0.0)
                a[q] = a[q] - factor * row_a
                b[q] = b[q] - factor * row_b
            yield
        if g < last:
            ahead = column[g + 1][8:]


def factor_steps(gram, result):
    size = gram.shape[0]
    tiles = lambda value: [value[8 * t : 8 * t + 8] for t in range(PANEL // 8)]
    row = lax.broadcasted_iota(jnp.int32, (size, size), 0)
    column = lax.broadcasted_iota(jnp.int32, (size, size), 1)
    other = jnp.where(row == column, 1.0, 0.0).astype(F32)
    uppers, inverses = [], []
    for start in range(0, size, PANEL):
        a, b = tiles(gram), tiles(other)
        yield from eliminate(a, b, start)
        a, b = jnp.concatenate(a, axis=0), jnp.concatenate(b, axis=0)
        here = row[start : start + PANEL]
        lanes = column[start : start + PANEL]
        scale = lax.rsqrt(jnp.sum(jnp.where(here == lanes, a, 0.0), axis=1, keepdims=True))
        upper, inverse = jnp.where(lanes >= here, a * scale, 0.0), b * scale
        uppers.append(upper)
        inverses.append(inverse)
        yield
        if start + PANEL < size:
            below = split(upper.T[start + PANEL :])
            change = dot_split(below, split(jnp.concatenate([upper, inverse], axis=1)))
            gram, other = gram[PANEL:] - change[:, :size], other[PANEL:] - change[:, size:]
        yield
    result += [jnp.concatenate(uppers, axis=0), jnp.concatenate(inverses, axis=0)]


def factorize(*grams):
    results = [[] for _ in grams]
    for _ in zip(*(factor_steps(gram, result) for gram, result in zip(grams, results, strict=True)), strict=True):
        pass
    return results


def self_products(terms):
    cross = dot(terms[1], terms[0], 1) + dot(terms[2], terms[0], 1)
    return dot(terms[0], terms[0], 1) + (cross + cross.T + dot(terms[1], terms[1], 1))


def grams_kernel(half_ref, ref, test_ref, grams_ref):
    columns = ref.shape[0] * LANES
    terms = split(jnp.concatenate([ref[b] for b in range(ref.shape[0])], axis=1))
    test = test_ref[pl.ds(pl.multiple_of(half_ref[0] * columns, columns), columns), :]
    grams_ref[0] = dot(terms[0], test) + (dot(terms[1], test) + dot(terms[2], test))
    grams_ref[1] = self_products(terms)


def half_grams(half, image, test_matrix):
    vmem = pl.BlockSpec(memory_space=pltpu.VMEM)
    return pl.pallas_call(
        grams_kernel,
        out_shape=pltpu.VMEM((2, LANES, LANES), F32),
        in_specs=[pl.BlockSpec(memory_space=pltpu.SMEM), vmem, vmem],
        out_specs=vmem,
        compiler_params=pltpu.CompilerParams(vmem_limit_bytes=VMEM_LIMIT),
        cost_estimate=pl.CostEstimate(flops=14 * LANES * image.size, bytes_accessed=4 * image.size, transcendentals=0),
        name="half_grams",
    )(half.reshape(1), image, test_matrix)


def finish_kernel(
    total_rows, place_ref, mine_grams, other_grams, mine_ref, other_ref, sketch_ref,
    basis_ref, right_ref, factor_ref, loadings, inverse_first, turned,
):
    blocks = mine_ref.shape[0]
    width = 2 * blocks * LANES
    core, own_block = place_ref[0], place_ref[1]

    def image_block(half, b):
        return jnp.where(core == half, mine_ref[b], other_ref[b])

    def write_right(inverse, block):
        turned[...] = dot_split(split(inverse), split(block)).T
        right_ref[...] = turned[pl.ds(pl.multiple_of(place_ref[2], 8), right_ref.shape[0]), :]

    gram = (mine_grams[0] + other_grams[0]) * (0.5 / total_rows)
    image_gram = (mine_grams[1] + other_grams[1]) * (1.0 / width)
    (_, inverse), (upper_image, inverse_image) = factorize(gram + gram.T, image_gram)
    left = split(inverse)
    inverse_first[...] = inverse
    basis_ref[...] = dot_split(split(sketch_ref[...]), left, 1)
    factor_ref[...] = dot_split(left, split(upper_image), 1)
    write_right(inverse_image, image_block(own_block // blocks, lax.rem(own_block, blocks)))

    row = lax.broadcasted_iota(jnp.int32, (LANES, LANES), 0)
    column = lax.broadcasted_iota(jnp.int32, (LANES, LANES), 1)
    trace = jnp.sum(jnp.where(row == column, image_gram, 0.0))
    spread = trace * jnp.sum(inverse_image * inverse_image)

    @pl.when(jnp.logical_not(spread <= SPREAD * LANES * LANES))
    def _():
        left = split(inverse_first[...])
        pair = jnp.concatenate([left[0], left[1]], axis=1)
        parts = []
        for half in range(2):
            x = split(jnp.concatenate([image_block(half, b) for b in range(blocks)], axis=1))
            values = dot(pair, jnp.concatenate([x[0], x[0]], axis=0)) + (
                dot(pair, jnp.concatenate([x[1], x[1]], axis=0))
                + dot(jnp.concatenate([left[2], left[0]], axis=1), jnp.concatenate([x[0], x[2]], axis=0))
            )
            for b in range(blocks):
                loadings[half * blocks + b] = values[:, b * LANES : (b + 1) * LANES]
            parts.append(self_products(split(values)))
        ((upper, second),) = factorize((parts[0] + parts[1]) * (1.0 / width))
        factor_ref[...] = upper.T
        write_right(second, loadings[own_block])


def finish(place, mine_grams, other_grams, mine, other, sketch, total_rows, own_rows):
    vmem = pl.BlockSpec(memory_space=pltpu.VMEM)
    return pl.pallas_call(
        functools.partial(finish_kernel, total_rows),
        out_shape=[
            jax.ShapeDtypeStruct(sketch.shape, F32),
            jax.ShapeDtypeStruct((own_rows, LANES), F32),
            jax.ShapeDtypeStruct((LANES, LANES), F32),
        ],
        in_specs=[pl.BlockSpec(memory_space=pltpu.SMEM)] + [vmem] * 5,
        out_specs=[vmem] * 3,
        scratch_shapes=[
            pltpu.VMEM((2 * mine.shape[0], LANES, LANES), F32),
            pltpu.VMEM((LANES, LANES), F32),
            pltpu.VMEM((LANES, LANES), F32),
        ],
        compiler_params=pltpu.CompilerParams(vmem_limit_bytes=VMEM_LIMIT),
        name="finish",
    )(place, mine_grams, other_grams, mine, other, sketch)


def exchange(values, axes):
    return lax.all_to_all(values, axes, 0, 0, tiled=False)


def scatter_sum(values, axes):
    parts = lax.axis_size(axes)
    blocks = values.reshape((parts, values.shape[0] // parts) + values.shape[1:])
    return jnp.sum(exchange(blocks, axes), axis=0)


def copies(values, axes):
    return exchange(jnp.broadcast_to(values[None], (lax.axis_size(axes),) + values.shape), axes)


def swap_cores(values):
    return lax.ppermute(values, "core", [(0, 1), (1, 0)])


def per_device(embeddings, test_matrix):
    devices_all = lax.axis_size(AXES)
    rows, width = embeddings.shape
    own_rows = width // devices_all
    core = lax.axis_index("core")
    sketch, send, keep_terms = local_sketch(core.reshape(1), embeddings, test_matrix)
    arriving = swap_cores(send)
    image = keep_image(sketch, keep_terms) + arriving
    piece = scatter_sum(image.reshape(-1, LANES), NEAR)
    piece = jnp.sum(copies(piece, "z_pair"), axis=0)
    mine = copies(piece, NEAR).reshape(image.shape)
    other = swap_cores(mine)
    mine_grams = half_grams(core, mine, test_matrix)
    other_grams = half_grams(1 - core, other, test_matrix)
    first = lax.axis_index(AXES) * own_rows
    place = jnp.stack([core, first // LANES, first % LANES])
    basis, right_basis, factor = finish(place, mine_grams, other_grams, mine, other, sketch, rows * devices_all, own_rows)
    return (basis, right_basis, factor)


def solution(mesh):
    fine = Mesh(mesh.devices.reshape(4, 8, 2, 2, 4), AXES)
    return jax.shard_map(
        per_device,
        mesh=fine,
        in_specs=(P(AXES, None), P()),
        out_specs=(P(AXES, None), P(AXES, None), P()),
        check_vma=False,
    )
```

```python
import functools

import jax
import jax.numpy as jnp
import numpy as np
from jax import lax
from jax.experimental import pallas as pl
from jax.experimental.pallas import tpu as pltpu
from jax.sharding import Mesh, PartitionSpec as P

AXES = ("y", "z_pair", "z_in_pair", "core", "x")
NEAR = ("z_in_pair", "x", "y")
BACK = ("x", "z_in_pair", "y")
CHUNKS = 4
STEP = 2048
PANEL = 32
SPREAD = 2.0
LANES = 128
F32, BF16 = jnp.float32, jnp.bfloat16
VMEM_LIMIT = 24 * 1024 * 1024


def dot(left, right, right_dim=0):
    return lax.dot_general(left, right, (((1,), (right_dim,)), ((), ())), preferred_element_type=F32)


def split(values):
    first = values.astype(BF16)
    rest = values - first.astype(F32)
    second = rest.astype(BF16)
    return first, second, (rest - second.astype(F32)).astype(BF16)


def dot_split(left, right, right_dim=0):
    return dot(left[0], right[0], right_dim) + (
        (dot(left[1], right[0], right_dim) + dot(left[0], right[1], right_dim))
        + (dot(left[2], right[0], right_dim) + dot(left[1], right[1], right_dim) + dot(left[0], right[2], right_dim))
    )


def image_pieces(left, right, out, first, slots):
    part = dot(left[0], right[0]) + (
        (dot(left[1], right[0]) + dot(left[0], right[1]))
        + (dot(left[2], right[0]) + dot(left[1], right[1]) + dot(left[0], right[2]))
    )
    height = out.shape[1]
    cuts = LANES // height
    for b in range(part.shape[1] // LANES):
        for h in range(cuts):
            out[slots[(first + b) * cuts + h]] = part[h * height : (h + 1) * height, b * LANES : (b + 1) * LANES]


def sketch_kernel(slots, core_ref, emb_hbm, test_hbm, sketch_ref, send_ref, keep_terms, emb, test, send_terms, sems):
    rows, width = emb.shape
    columns = width // CHUNKS
    core = core_ref[0]
    copies = []
    for c in range(CHUNKS):
        there = pl.multiple_of(lax.rem(core * (width // 2) + c * columns, width), columns)
        here = pl.ds(c * columns, columns)
        copies.append(
            (
                pltpu.make_async_copy(emb_hbm.at[:, pl.ds(there, columns)], emb.at[:, here], sems.at[0, c]),
                pltpu.make_async_copy(test_hbm.at[pl.ds(there, columns)], test.at[here], sems.at[1, c]),
            )
        )
    for pair in copies:
        for copy in pair:
            copy.start()
    sketch = jnp.zeros((rows, LANES), F32)
    for c in range(CHUNKS):
        for copy in copies[c]:
            copy.wait()
        here = slice(c * columns, (c + 1) * columns)
        parts = split(emb[:, here])
        terms, first = (keep_terms, 0) if c < CHUNKS // 2 else (send_terms, width // 2)
        for t in range(3):
            terms[t, :, here.start - first : here.stop - first] = parts[t]
            sketch += dot(parts[t], test[here])
    sketch_ref[...] = sketch
    left = split(sketch.T)
    for start in range(0, width // 2, STEP):
        right = [send_terms[t, :, start : start + STEP] for t in range(3)]
        image_pieces(left, right, send_ref, start // LANES, slots)


def keep_kernel(slots, sketch_ref, keep_terms, keep_ref):
    left = split(sketch_ref[...].T)
    for start in range(0, keep_terms.shape[2], STEP):
        right = [keep_terms[t, :, start : start + STEP] for t in range(3)]
        image_pieces(left, right, keep_ref, start // LANES, slots)


def local_sketch(core, embeddings, test_matrix, slots):
    rows, width = embeddings.shape
    half = width // 2
    vmem = pl.BlockSpec(memory_space=pltpu.VMEM)
    return pl.pallas_call(
        functools.partial(sketch_kernel, slots),
        out_shape=[
            pltpu.VMEM((rows, LANES), F32),
            pltpu.VMEM((len(slots), half // len(slots), LANES), F32),
            pltpu.VMEM((3, rows, half), BF16),
        ],
        in_specs=[
            pl.BlockSpec(memory_space=pltpu.SMEM),
            pl.BlockSpec(memory_space=pltpu.HBM),
            pl.BlockSpec(memory_space=pltpu.HBM),
        ],
        out_specs=[vmem] * 3,
        scratch_shapes=[
            pltpu.VMEM((rows, width), F32),
            pltpu.VMEM((width, LANES), BF16),
            pltpu.VMEM((3, rows, half), BF16),
            pltpu.SemaphoreType.DMA((2, CHUNKS)),
        ],
        compiler_params=pltpu.CompilerParams(vmem_limit_bytes=VMEM_LIMIT),
        cost_estimate=pl.CostEstimate(flops=12 * rows * width * LANES, bytes_accessed=4 * rows * width, transcendentals=0),
        name="local_sketch",
    )(
        core,
        pltpu.with_memory_space_constraint(embeddings, pltpu.HBM),
        pltpu.with_memory_space_constraint(test_matrix, pltpu.HBM),
    )


def keep_image(sketch, keep_terms, slots):
    rows, half = keep_terms.shape[1:]
    vmem = pl.BlockSpec(memory_space=pltpu.VMEM)
    return pl.pallas_call(
        functools.partial(keep_kernel, slots),
        out_shape=pltpu.VMEM((len(slots), half // len(slots), LANES), F32),
        in_specs=[vmem] * 2,
        out_specs=vmem,
        compiler_params=pltpu.CompilerParams(vmem_limit_bytes=VMEM_LIMIT),
        cost_estimate=pl.CostEstimate(flops=12 * rows * half * LANES, bytes_accessed=6 * rows * half, transcendentals=0),
        name="keep_image",
    )(sketch, keep_terms)


def over_sublanes(tile, row):
    return jnp.broadcast_to(tile[row : row + 1], tile.shape)


def over_lanes(tile, lane):
    return jnp.broadcast_to(tile[:, lane : lane + 1], tile.shape)


def eliminate(a, b, first_lane):
    sublane = lax.broadcasted_iota(jnp.int32, (8, LANES), 0)
    spread = lambda tile, first: [over_lanes(tile, first + k) for k in range(8)]
    last = len(a) - 1
    ahead = spread(a[0], first_lane)
    for g in range(last + 1):
        first = first_lane + 8 * g
        column = {q: spread(a[q], first) for q in range(g + 1, last + 1)}
        column[g] = ahead
        if g < last:
            column[g] = column[g] + spread(a[g], first + 8)
            column[g + 1] = column[g + 1] + spread(a[g + 1], first + 8)
        for i in range(8):
            pivots = [over_sublanes(values, i) for values in column[g]]
            inverse = 1.0 / pivots[i]
            row_a, row_b = over_sublanes(a[g], i), over_sublanes(b[g], i)
            for q in range(g, last + 1):
                factor = column[q][i] * inverse
                for k in range(i + 1, len(column[q])):
                    column[q][k] = column[q][k] - factor * pivots[k]
                if q == g:
                    factor = jnp.where(sublane > i, factor, 0.0)
                a[q] = a[q] - factor * row_a
                b[q] = b[q] - factor * row_b
            yield
        if g < last:
            ahead = column[g + 1][8:]


def factor_steps(gram, result):
    size = gram.shape[0]
    tiles = lambda value: [value[8 * t : 8 * t + 8] for t in range(PANEL // 8)]
    row = lax.broadcasted_iota(jnp.int32, (size, size), 0)
    column = lax.broadcasted_iota(jnp.int32, (size, size), 1)
    other = jnp.where(row == column, 1.0, 0.0).astype(F32)
    uppers, inverses = [], []
    for start in range(0, size, PANEL):
        a, b = tiles(gram), tiles(other)
        yield from eliminate(a, b, start)
        a, b = jnp.concatenate(a, axis=0), jnp.concatenate(b, axis=0)
        here = row[start : start + PANEL]
        lanes = column[start : start + PANEL]
        scale = lax.rsqrt(jnp.sum(jnp.where(here == lanes, a, 0.0), axis=1, keepdims=True))
        upper, inverse = jnp.where(lanes >= here, a * scale, 0.0), b * scale
        uppers.append(upper)
        inverses.append(inverse)
        yield
        if start + PANEL < size:
            below = split(upper.T[start + PANEL :])
            change = dot_split(below, split(jnp.concatenate([upper, inverse], axis=1)))
            gram, other = gram[PANEL:] - change[:, :size], other[PANEL:] - change[:, size:]
        yield
    result += [jnp.concatenate(uppers, axis=0), jnp.concatenate(inverses, axis=0)]


def factorize(*grams):
    results = [[] for _ in grams]
    for _ in zip(*(factor_steps(gram, result) for gram, result in zip(grams, results, strict=True)), strict=True):
        pass
    return results


def self_products(terms):
    cross = dot(terms[1], terms[0], 1) + dot(terms[2], terms[0], 1)
    return dot(terms[0], terms[0], 1) + (cross + cross.T + dot(terms[1], terms[1], 1))


def grams_kernel(half_ref, ref, test_ref, grams_ref):
    columns = ref.shape[0] * LANES
    terms = split(jnp.concatenate([ref[b] for b in range(ref.shape[0])], axis=1))
    test = test_ref[pl.ds(pl.multiple_of(half_ref[0] * columns, columns), columns), :]
    grams_ref[0] = dot(terms[0], test) + (dot(terms[1], test) + dot(terms[2], test))
    grams_ref[1] = self_products(terms)


def half_grams(half, image, test_matrix):
    vmem = pl.BlockSpec(memory_space=pltpu.VMEM)
    return pl.pallas_call(
        grams_kernel,
        out_shape=pltpu.VMEM((2, LANES, LANES), F32),
        in_specs=[pl.BlockSpec(memory_space=pltpu.SMEM), vmem, vmem],
        out_specs=vmem,
        compiler_params=pltpu.CompilerParams(vmem_limit_bytes=VMEM_LIMIT),
        cost_estimate=pl.CostEstimate(flops=14 * LANES * image.size, bytes_accessed=4 * image.size, transcendentals=0),
        name="half_grams",
    )(half.reshape(1), image, test_matrix)


def finish_kernel(
    total_rows, place_ref, mine_grams, other_grams, mine_ref, other_ref, sketch_ref,
    basis_ref, right_ref, factor_ref, loadings, inverse_first, turned,
):
    blocks = mine_ref.shape[0]
    width = 2 * blocks * LANES
    core, own_block = place_ref[0], place_ref[1]

    def image_block(half, b):
        return jnp.where(core == half, mine_ref[b], other_ref[b])

    def write_right(inverse, block):
        turned[...] = dot_split(split(inverse), split(block)).T
        right_ref[...] = turned[pl.ds(pl.multiple_of(place_ref[2], 8), right_ref.shape[0]), :]

    gram = (mine_grams[0] + other_grams[0]) * (0.5 / total_rows)
    image_gram = (mine_grams[1] + other_grams[1]) * (1.0 / width)
    (_, inverse), (upper_image, inverse_image) = factorize(gram + gram.T, image_gram)
    left = split(inverse)
    inverse_first[...] = inverse
    basis_ref[...] = dot_split(split(sketch_ref[...]), left, 1)
    factor_ref[...] = dot_split(left, split(upper_image), 1)
    write_right(inverse_image, image_block(own_block // blocks, lax.rem(own_block, blocks)))

    row = lax.broadcasted_iota(jnp.int32, (LANES, LANES), 0)
    column = lax.broadcasted_iota(jnp.int32, (LANES, LANES), 1)
    trace = jnp.sum(jnp.where(row == column, image_gram, 0.0))
    spread = trace * jnp.sum(inverse_image * inverse_image)

    @pl.when(jnp.logical_not(spread <= SPREAD * LANES * LANES))
    def _():
        left = split(inverse_first[...])
        pair = jnp.concatenate([left[0], left[1]], axis=1)
        parts = []
        for half in range(2):
            x = split(jnp.concatenate([image_block(half, b) for b in range(blocks)], axis=1))
            values = dot(pair, jnp.concatenate([x[0], x[0]], axis=0)) + (
                dot(pair, jnp.concatenate([x[1], x[1]], axis=0))
                + dot(jnp.concatenate([left[2], left[0]], axis=1), jnp.concatenate([x[0], x[2]], axis=0))
            )
            for b in range(blocks):
                loadings[half * blocks + b] = values[:, b * LANES : (b + 1) * LANES]
            parts.append(self_products(split(values)))
        ((upper, second),) = factorize((parts[0] + parts[1]) * (1.0 / width))
        factor_ref[...] = upper.T
        write_right(second, loadings[own_block])


def finish(place, mine_grams, other_grams, mine, other, sketch, total_rows, own_rows):
    vmem = pl.BlockSpec(memory_space=pltpu.VMEM)
    return pl.pallas_call(
        functools.partial(finish_kernel, total_rows),
        out_shape=[
            jax.ShapeDtypeStruct(sketch.shape, F32),
            jax.ShapeDtypeStruct((own_rows, LANES), F32),
            jax.ShapeDtypeStruct((LANES, LANES), F32),
        ],
        in_specs=[pl.BlockSpec(memory_space=pltpu.SMEM)] + [vmem] * 5,
        out_specs=[vmem] * 3,
        scratch_shapes=[
            pltpu.VMEM((2 * mine.shape[0], LANES, LANES), F32),
            pltpu.VMEM((LANES, LANES), F32),
            pltpu.VMEM((LANES, LANES), F32),
        ],
        compiler_params=pltpu.CompilerParams(vmem_limit_bytes=VMEM_LIMIT),
        name="finish",
    )(place, mine_grams, other_grams, mine, other, sketch)


def exchange(values, axes):
    return lax.all_to_all(values, axes, 0, 0, tiled=False)


def slots_of_pieces():
    sizes = [lax.axis_size(axis) for axis in BACK]
    order = [BACK.index(axis) for axis in NEAR]
    places = np.arange(np.prod(sizes)).reshape([sizes[i] for i in order])
    return [int(place) for place in places.transpose(np.argsort(order)).reshape(-1)]


def copies(values, axes):
    return exchange(jnp.broadcast_to(values[None], (lax.axis_size(axes),) + values.shape), axes)


def swap_cores(values):
    return lax.ppermute(values, "core", [(0, 1), (1, 0)])


def per_device(embeddings, test_matrix):
    devices_all = lax.axis_size(AXES)
    rows, width = embeddings.shape
    own_rows = width // devices_all
    core = lax.axis_index("core")
    slots = slots_of_pieces()
    sketch, send, keep_terms = local_sketch(core.reshape(1), embeddings, test_matrix, slots)
    arriving = swap_cores(send)
    image = keep_image(sketch, keep_terms, slots) + arriving
    piece = jnp.sum(exchange(image, NEAR), axis=0)
    piece = jnp.sum(copies(piece, "z_pair"), axis=0)
    mine = copies(piece, BACK).reshape(-1, LANES, LANES)
    other = swap_cores(mine)
    mine_grams = half_grams(core, mine, test_matrix)
    other_grams = half_grams(1 - core, other, test_matrix)
    first = lax.axis_index(AXES) * own_rows
    place = jnp.stack([core, first // LANES, first % LANES])
    basis, right_basis, factor = finish(place, mine_grams, other_grams, mine, other, sketch, rows * devices_all, own_rows)
    return (basis, right_basis, factor)


def solution(mesh):
    fine = Mesh(mesh.devices.reshape(4, 8, 2, 2, 4), AXES)
    return jax.shard_map(
        per_device,
        mesh=fine,
        in_specs=(P(AXES, None), P()),
        out_specs=(P(AXES, None), P(AXES, None), P()),
        check_vma=False,
    )
```

```python
import functools

import jax
import jax.numpy as jnp
import numpy as np
from jax import lax
from jax.experimental import pallas as pl
from jax.experimental.pallas import tpu as pltpu
from jax.sharding import Mesh, PartitionSpec as P

AXES = ("y", "z_half", "z_pair", "z_in_pair", "core", "x")
FAR = ("z_pair", "z_half")
NEAR = ("z_in_pair", "x", "y")
BACK = ("x", "z_in_pair", "y")
CHUNKS = 4
STEP = 2048
PANEL = 32
SPREAD = 2.0
LANES = 128
F32, BF16 = jnp.float32, jnp.bfloat16
VMEM_LIMIT = 24 * 1024 * 1024


def dot(left, right, right_dim=0):
    return lax.dot_general(left, right, (((1,), (right_dim,)), ((), ())), preferred_element_type=F32)


def split(values):
    first = values.astype(BF16)
    rest = values - first.astype(F32)
    second = rest.astype(BF16)
    return first, second, (rest - second.astype(F32)).astype(BF16)


def dot_split(left, right, right_dim=0):
    return dot(left[0], right[0], right_dim) + (
        (dot(left[1], right[0], right_dim) + dot(left[0], right[1], right_dim))
        + (dot(left[2], right[0], right_dim) + dot(left[1], right[1], right_dim) + dot(left[0], right[2], right_dim))
    )


def image_pieces(left, right, out, first, slots):
    part = dot(left[0], right[0]) + (
        (dot(left[1], right[0]) + dot(left[0], right[1]))
        + (dot(left[2], right[0]) + dot(left[1], right[1]) + dot(left[0], right[2]))
    )
    height = out.shape[1]
    cuts = LANES // height
    for b in range(part.shape[1] // LANES):
        for h in range(cuts):
            out[slots[(first + b) * cuts + h]] = part[h * height : (h + 1) * height, b * LANES : (b + 1) * LANES]


def sketch_kernel(slots, core_ref, emb_hbm, test_hbm, sketch_ref, send_ref, keep_terms, emb, test, send_terms, sems):
    rows, width = emb.shape
    columns = width // CHUNKS
    core = core_ref[0]
    copies = []
    for c in range(CHUNKS):
        there = pl.multiple_of(lax.rem(core * (width // 2) + c * columns, width), columns)
        here = pl.ds(c * columns, columns)
        copies.append(
            (
                pltpu.make_async_copy(emb_hbm.at[:, pl.ds(there, columns)], emb.at[:, here], sems.at[0, c]),
                pltpu.make_async_copy(test_hbm.at[pl.ds(there, columns)], test.at[here], sems.at[1, c]),
            )
        )
    for pair in copies:
        for copy in pair:
            copy.start()
    sketch = jnp.zeros((rows, LANES), F32)
    for c in range(CHUNKS):
        for copy in copies[c]:
            copy.wait()
        here = slice(c * columns, (c + 1) * columns)
        parts = split(emb[:, here])
        terms, first = (keep_terms, 0) if c < CHUNKS // 2 else (send_terms, width // 2)
        for t in range(3):
            terms[t, :, here.start - first : here.stop - first] = parts[t]
            sketch += dot(parts[t], test[here])
    sketch_ref[...] = sketch
    left = split(sketch.T)
    for start in range(0, width // 2, STEP):
        right = [send_terms[t, :, start : start + STEP] for t in range(3)]
        image_pieces(left, right, send_ref, start // LANES, slots)


def keep_kernel(slots, sketch_ref, keep_terms, keep_ref):
    left = split(sketch_ref[...].T)
    for start in range(0, keep_terms.shape[2], STEP):
        right = [keep_terms[t, :, start : start + STEP] for t in range(3)]
        image_pieces(left, right, keep_ref, start // LANES, slots)


def local_sketch(core, embeddings, test_matrix, slots):
    rows, width = embeddings.shape
    half = width // 2
    vmem = pl.BlockSpec(memory_space=pltpu.VMEM)
    return pl.pallas_call(
        functools.partial(sketch_kernel, slots),
        out_shape=[
            pltpu.VMEM((rows, LANES), F32),
            pltpu.VMEM((len(slots), half // len(slots), LANES), F32),
            pltpu.VMEM((3, rows, half), BF16),
        ],
        in_specs=[
            pl.BlockSpec(memory_space=pltpu.SMEM),
            pl.BlockSpec(memory_space=pltpu.HBM),
            pl.BlockSpec(memory_space=pltpu.HBM),
        ],
        out_specs=[vmem] * 3,
        scratch_shapes=[
            pltpu.VMEM((rows, width), F32),
            pltpu.VMEM((width, LANES), BF16),
            pltpu.VMEM((3, rows, half), BF16),
            pltpu.SemaphoreType.DMA((2, CHUNKS)),
        ],
        compiler_params=pltpu.CompilerParams(vmem_limit_bytes=VMEM_LIMIT),
        cost_estimate=pl.CostEstimate(flops=12 * rows * width * LANES, bytes_accessed=4 * rows * width, transcendentals=0),
        name="local_sketch",
    )(
        core,
        pltpu.with_memory_space_constraint(embeddings, pltpu.HBM),
        pltpu.with_memory_space_constraint(test_matrix, pltpu.HBM),
    )


def keep_image(sketch, keep_terms, slots):
    rows, half = keep_terms.shape[1:]
    vmem = pl.BlockSpec(memory_space=pltpu.VMEM)
    return pl.pallas_call(
        functools.partial(keep_kernel, slots),
        out_shape=pltpu.VMEM((len(slots), half // len(slots), LANES), F32),
        in_specs=[vmem] * 2,
        out_specs=vmem,
        compiler_params=pltpu.CompilerParams(vmem_limit_bytes=VMEM_LIMIT),
        cost_estimate=pl.CostEstimate(flops=12 * rows * half * LANES, bytes_accessed=6 * rows * half, transcendentals=0),
        name="keep_image",
    )(sketch, keep_terms)


def over_sublanes(tile, row):
    return jnp.broadcast_to(tile[row : row + 1], tile.shape)


def over_lanes(tile, lane):
    return jnp.broadcast_to(tile[:, lane : lane + 1], tile.shape)


def eliminate(a, b, first_lane):
    sublane = lax.broadcasted_iota(jnp.int32, (8, LANES), 0)
    spread = lambda tile, first: [over_lanes(tile, first + k) for k in range(8)]
    last = len(a) - 1
    ahead = spread(a[0], first_lane)
    for g in range(last + 1):
        first = first_lane + 8 * g
        column = {q: spread(a[q], first) for q in range(g + 1, last + 1)}
        column[g] = ahead
        if g < last:
            column[g] = column[g] + spread(a[g], first + 8)
            column[g + 1] = column[g + 1] + spread(a[g + 1], first + 8)
        for i in range(8):
            pivots = [over_sublanes(values, i) for values in column[g]]
            inverse = 1.0 / pivots[i]
            row_a, row_b = over_sublanes(a[g], i), over_sublanes(b[g], i)
            for q in range(g, last + 1):
                factor = column[q][i] * inverse
                for k in range(i + 1, len(column[q])):
                    column[q][k] = column[q][k] - factor * pivots[k]
                if q == g:
                    factor = jnp.where(sublane > i, factor, 0.0)
                a[q] = a[q] - factor * row_a
                b[q] = b[q] - factor * row_b
            yield
        if g < last:
            ahead = column[g + 1][8:]


def factor_steps(gram, result):
    size = gram.shape[0]
    tiles = lambda value: [value[8 * t : 8 * t + 8] for t in range(PANEL // 8)]
    row = lax.broadcasted_iota(jnp.int32, (size, size), 0)
    column = lax.broadcasted_iota(jnp.int32, (size, size), 1)
    other = jnp.where(row == column, 1.0, 0.0).astype(F32)
    uppers, inverses = [], []
    for start in range(0, size, PANEL):
        a, b = tiles(gram), tiles(other)
        yield from eliminate(a, b, start)
        a, b = jnp.concatenate(a, axis=0), jnp.concatenate(b, axis=0)
        here = row[start : start + PANEL]
        lanes = column[start : start + PANEL]
        scale = lax.rsqrt(jnp.sum(jnp.where(here == lanes, a, 0.0), axis=1, keepdims=True))
        upper, inverse = jnp.where(lanes >= here, a * scale, 0.0), b * scale
        uppers.append(upper)
        inverses.append(inverse)
        yield
        if start + PANEL < size:
            below = split(upper.T[start + PANEL :])
            change = dot_split(below, split(jnp.concatenate([upper, inverse], axis=1)))
            gram, other = gram[PANEL:] - change[:, :size], other[PANEL:] - change[:, size:]
        yield
    result += [jnp.concatenate(uppers, axis=0), jnp.concatenate(inverses, axis=0)]


def factorize(*grams):
    results = [[] for _ in grams]
    for _ in zip(*(factor_steps(gram, result) for gram, result in zip(grams, results, strict=True)), strict=True):
        pass
    return results


def self_products(terms):
    cross = dot(terms[1], terms[0], 1) + dot(terms[2], terms[0], 1)
    return dot(terms[0], terms[0], 1) + (cross + cross.T + dot(terms[1], terms[1], 1))


def grams_kernel(half_ref, ref, test_ref, grams_ref):
    columns = ref.shape[0] * LANES
    terms = split(jnp.concatenate([ref[b] for b in range(ref.shape[0])], axis=1))
    test = test_ref[pl.ds(pl.multiple_of(half_ref[0] * columns, columns), columns), :]
    grams_ref[0] = dot(terms[0], test) + (dot(terms[1], test) + dot(terms[2], test))
    grams_ref[1] = self_products(terms)


def half_grams(half, image, test_matrix):
    vmem = pl.BlockSpec(memory_space=pltpu.VMEM)
    return pl.pallas_call(
        grams_kernel,
        out_shape=pltpu.VMEM((2, LANES, LANES), F32),
        in_specs=[pl.BlockSpec(memory_space=pltpu.SMEM), vmem, vmem],
        out_specs=vmem,
        compiler_params=pltpu.CompilerParams(vmem_limit_bytes=VMEM_LIMIT),
        cost_estimate=pl.CostEstimate(flops=14 * LANES * image.size, bytes_accessed=4 * image.size, transcendentals=0),
        name="half_grams",
    )(half.reshape(1), image, test_matrix)


def finish_kernel(
    total_rows, place_ref, mine_grams, other_grams, mine_ref, other_ref, sketch_ref,
    basis_ref, right_ref, factor_ref, loadings, inverse_first, turned,
):
    blocks = mine_ref.shape[0]
    width = 2 * blocks * LANES
    core, own_block = place_ref[0], place_ref[1]

    def image_block(half, b):
        return jnp.where(core == half, mine_ref[b], other_ref[b])

    def write_right(inverse, block):
        turned[...] = dot_split(split(inverse), split(block)).T
        right_ref[...] = turned[pl.ds(pl.multiple_of(place_ref[2], 8), right_ref.shape[0]), :]

    gram = (mine_grams[0] + other_grams[0]) * (0.5 / total_rows)
    image_gram = (mine_grams[1] + other_grams[1]) * (1.0 / width)
    (_, inverse), (upper_image, inverse_image) = factorize(gram + gram.T, image_gram)
    left = split(inverse)
    inverse_first[...] = inverse
    basis_ref[...] = dot_split(split(sketch_ref[...]), left, 1)
    factor_ref[...] = dot_split(left, split(upper_image), 1)
    write_right(inverse_image, image_block(own_block // blocks, lax.rem(own_block, blocks)))

    row = lax.broadcasted_iota(jnp.int32, (LANES, LANES), 0)
    column = lax.broadcasted_iota(jnp.int32, (LANES, LANES), 1)
    trace = jnp.sum(jnp.where(row == column, image_gram, 0.0))
    spread = trace * jnp.sum(inverse_image * inverse_image)

    @pl.when(jnp.logical_not(spread <= SPREAD * LANES * LANES))
    def _():
        left = split(inverse_first[...])
        pair = jnp.concatenate([left[0], left[1]], axis=1)
        parts = []
        for half in range(2):
            x = split(jnp.concatenate([image_block(half, b) for b in range(blocks)], axis=1))
            values = dot(pair, jnp.concatenate([x[0], x[0]], axis=0)) + (
                dot(pair, jnp.concatenate([x[1], x[1]], axis=0))
                + dot(jnp.concatenate([left[2], left[0]], axis=1), jnp.concatenate([x[0], x[2]], axis=0))
            )
            for b in range(blocks):
                loadings[half * blocks + b] = values[:, b * LANES : (b + 1) * LANES]
            parts.append(self_products(split(values)))
        ((upper, second),) = factorize((parts[0] + parts[1]) * (1.0 / width))
        factor_ref[...] = upper.T
        write_right(second, loadings[own_block])


def finish(place, mine_grams, other_grams, mine, other, sketch, total_rows, own_rows):
    vmem = pl.BlockSpec(memory_space=pltpu.VMEM)
    return pl.pallas_call(
        functools.partial(finish_kernel, total_rows),
        out_shape=[
            jax.ShapeDtypeStruct(sketch.shape, F32),
            jax.ShapeDtypeStruct((own_rows, LANES), F32),
            jax.ShapeDtypeStruct((LANES, LANES), F32),
        ],
        in_specs=[pl.BlockSpec(memory_space=pltpu.SMEM)] + [vmem] * 5,
        out_specs=[vmem] * 3,
        scratch_shapes=[
            pltpu.VMEM((2 * mine.shape[0], LANES, LANES), F32),
            pltpu.VMEM((LANES, LANES), F32),
            pltpu.VMEM((LANES, LANES), F32),
        ],
        compiler_params=pltpu.CompilerParams(vmem_limit_bytes=VMEM_LIMIT),
        name="finish",
    )(place, mine_grams, other_grams, mine, other, sketch)


def exchange(values, axes):
    return lax.all_to_all(values, axes, 0, 0, tiled=False)


def slots_of_pieces():
    sizes = [lax.axis_size(axis) for axis in BACK]
    order = [BACK.index(axis) for axis in NEAR]
    places = np.arange(np.prod(sizes)).reshape([sizes[i] for i in order])
    return [int(place) for place in places.transpose(np.argsort(order)).reshape(-1)]


def copies(values, axes):
    return exchange(jnp.broadcast_to(values[None], (lax.axis_size(axes),) + values.shape), axes)


def swap_cores(values):
    return lax.ppermute(values, "core", [(0, 1), (1, 0)])


def per_device(embeddings, test_matrix):
    devices_all = lax.axis_size(AXES)
    rows, width = embeddings.shape
    own_rows = width // devices_all
    core = lax.axis_index("core")
    slots = slots_of_pieces()
    sketch, send, keep_terms = local_sketch(core.reshape(1), embeddings, test_matrix, slots)
    arriving = swap_cores(send)
    image = keep_image(sketch, keep_terms, slots) + arriving
    piece = jnp.sum(exchange(image, NEAR), axis=0)
    piece = jnp.sum(copies(piece, FAR), axis=0)
    mine = copies(piece, BACK).reshape(-1, LANES, LANES)
    other = swap_cores(mine)
    mine_grams = half_grams(core, mine, test_matrix)
    other_grams = half_grams(1 - core, other, test_matrix)
    first = lax.axis_index(AXES) * own_rows
    place = jnp.stack([core, first // LANES, first % LANES])
    basis, right_basis, factor = finish(place, mine_grams, other_grams, mine, other, sketch, rows * devices_all, own_rows)
    return (basis, right_basis, factor)


def solution(mesh):
    fine = Mesh(mesh.devices.reshape(4, 2, 4, 2, 2, 4), AXES)
    return jax.shard_map(
        per_device,
        mesh=fine,
        in_specs=(P(AXES, None), P()),
        out_specs=(P(AXES, None), P(AXES, None), P()),
        check_vma=False,
    )
```
